256 devices in a mesh: rep: 32 (over z, y_hi, core), fsdp: 8 (over y_lo, x).
Axes of the slice: x: 4, y: 4 (y_hi: 2, y_lo: 2; y = y_hi * 2 + y_lo), z: 8, core: 2. Of those that a mesh axis runs over, the one named last changes fastest.
Arguments:
- latent_tokens: bfloat16 [32, 4096, 4096], P('rep', 'fsdp'), may hold values from -6 to 6
- actions: int32 [32, 16], P('rep'), may hold values from 0 to 7
- action_table: bfloat16 [8, 4096], replicated, may hold values from -6 to 6
- key_value_weight: bfloat16 [32, 4096, 1024], P('rep', 'fsdp'), may hold values from -0.09375 to 0.09375
- queries: bfloat16 [32, 4096, 2048], P('rep', 'fsdp'), may hold values from -6 to 6
- output_cotangent: bfloat16 [32, 4096, 2048], P('rep', 'fsdp'), may hold values from -0.09375 to 0.09375
- outer_delta: float32 [32, 256, 4096], P('rep', 'fsdp'), may hold values from -6 to 6
- momentum: float32 [256, 4096], P('fsdp'), may hold values from -6 to 6
- anchor: float32 [256, 4096], P('fsdp'), may hold values from -6 to 6
Outputs:
- weight_gradient: bfloat16 [32, 4096, 1024], P('rep', 'fsdp')
- new_momentum: float32 [256, 4096], P('fsdp')
- new_anchor: float32 [256, 4096], P('fsdp')
The draws below stay inside these ranges and needn't reach their ends.
All inputs are finite; a program needn't handle non-finite values.
Results may differ from the reference program's by a relative error of at most 0.019.
Values may be sent and summed in bfloat16 or wider, within the bound.
A program may use at most 128 MiB of HBM per device.

```python
import jax
import jax.numpy as jnp
from jax import lax

D = 4096
HEAD_DIM = 128
KV_HEADS = 4
GROUP = 4
ACTIONS = 8
FRAMES = 16
TOKENS = 4096
QW = 2048
KVW = 1024
FRAG_ROWS = 256
N_REP = 32


def plant(array, own_key, smallest, high):
    dims = array.shape
    spot = [jax.random.randint(jax.random.fold_in(own_key, axis), (), 0, dims[axis]) for axis in range(len(dims))]
    array = array.at[tuple(spot)].set(smallest)
    longest = dims.index(max(dims))
    spot[longest] = (spot[longest] + 1) % dims[longest]
    return array.at[tuple(spot)].set(high)


def raised(entries, stream_key, source, target, shards_of, factor):
    def block_of(axis_at):
        return (jnp.arange(entries.shape[axis_at]) // (entries.shape[axis_at] // shards_of)).reshape((-1,) + (1,) * (entries.ndim - 1 - axis_at))

    near = jax.random.permutation(stream_key, shards_of)[block_of(target)]
    far = (block_of(target) + shards_of // 2) % shards_of
    return jnp.where((block_of(source) == near) | (block_of(source) == far), factor * entries, entries)


def level_of(own_key, shape, pieces, smallest, largest):
    loudness = 1.0
    for position, blocks in pieces:
        heights = jax.random.uniform(jax.random.fold_in(jax.random.fold_in(own_key, 6), position), (blocks,), jnp.float32, smallest / len(pieces), largest / len(pieces))
        loudness = loudness * jnp.repeat(jnp.exp(heights), shape[position] // blocks).reshape((-1,) + (1,) * (len(shape) - 1 - position))
    return loudness


def gaussian(own_key, extent, deviation, reach, split=(), kind=jnp.bfloat16):
    factor_of = level_of(own_key, extent, split, -0.22, 0.18) if split else 1.0
    drawn = jax.random.normal(own_key, extent, jnp.float32) * deviation * factor_of
    return jnp.minimum(jnp.maximum(drawn, -reach), reach).astype(kind)


def heavy_noise(key, dims, deviation, reach, cuts, heavy, kind=jnp.bfloat16):
    entries = deviation * jax.random.normal(key, dims, jnp.float32)
    if cuts:
        entries = entries * level_of(key, dims, cuts, -0.22, 0.18)
    return jnp.clip(raised(entries, jax.random.fold_in(key, 3), *heavy), -reach, reach).astype(kind)


def setup_inputs(seed: int = 0) -> dict:
    key_of = jax.random.split(jax.random.key(seed), 10)
    latent_tokens = gaussian(key_of[0], (N_REP, TOKENS, D), 1.0, 6.0, ((0, 32), (1, 8)))
    actions = plant(jax.random.randint(key_of[1], (N_REP, FRAMES), 0, ACTIONS), jax.random.fold_in(key_of[1], 1), 0, ACTIONS - 1).astype(jnp.int32)
    action_table = gaussian(key_of[2], (ACTIONS, D), 1.0, 6.0)
    key_value_weight = gaussian(key_of[3], (N_REP, D, KVW), D ** -0.5, 0.09375, ((0, 32), (1, 8)))
    queries = gaussian(key_of[4], (N_REP, TOKENS, QW), 1.0, 6.0, ((0, 32), (1, 8)))
    output_cotangent = gaussian(key_of[5], (N_REP, TOKENS, QW), (TOKENS ** -0.5), 0.09375, ((0, 32), (1, 8)))
    outer_delta = heavy_noise(key_of[6], (N_REP, FRAG_ROWS, D), 1.0, 6.0, ((0, 32), (1, 8)), (0, 1, 32, 2.75), jnp.float32)
    momentum = gaussian(key_of[7], (FRAG_ROWS, D), 1.0, 6.0, ((0, 8),), jnp.float32)
    anchor = gaussian(key_of[8], (FRAG_ROWS, D), 1.0, 6.0, ((0, 8),), jnp.float32)
    return dict(latent_tokens=latent_tokens, actions=actions, action_table=action_table, key_value_weight=key_value_weight, queries=queries, output_cotangent=output_cotangent, outer_delta=outer_delta, momentum=momentum, anchor=anchor)


MOMENTUM_RATE = 0.9
OUTER_RATE = 0.7

def condition(latents, frame_actions, action_table):
    token_count = latents.shape[0]
    patch_count = token_count // FRAMES
    one_hot = (frame_actions[:, None] == jnp.arange(ACTIONS, dtype=jnp.int32)[None, :]).astype(jnp.bfloat16)
    frame_embed = jnp.dot(one_hot, action_table, preferred_element_type=jnp.float32)
    summed = latents.astype(jnp.float32).reshape(patch_count, FRAMES, -1) + frame_embed[None]
    return summed.reshape(token_count, -1).astype(jnp.bfloat16)

def attention_grad(key_value, query_rows, cotangent):
    token_count = query_rows.shape[0]
    patch_count = token_count // FRAMES
    split_at = KV_HEADS * HEAD_DIM
    wide = key_value.astype(jnp.float32)
    key_heads = wide[:, :split_at].reshape(patch_count, FRAMES, KV_HEADS, HEAD_DIM)
    value_heads = wide[:, split_at:].reshape(patch_count, FRAMES, KV_HEADS, HEAD_DIM)
    query_heads = query_rows.astype(jnp.float32).reshape(patch_count, FRAMES, KV_HEADS, GROUP, HEAD_DIM)
    upstream = cotangent.astype(jnp.float32).reshape(patch_count, FRAMES, KV_HEADS, GROUP, HEAD_DIM)
    score_scale = HEAD_DIM ** (-0.5)
    scores = jnp.einsum('pfkgd,ptkd->pkgft', query_heads, key_heads) * score_scale
    frame_index = jnp.arange(FRAMES, dtype=jnp.int32)
    causal = frame_index[None, :] <= frame_index[:, None]
    exp_scores = jnp.where(causal, jnp.exp(scores), jnp.float32(0.0))
    probabilities = exp_scores / lax.optimization_barrier(jnp.sum(exp_scores, axis=-1, keepdims=True))
    probs_low = lax.optimization_barrier(probabilities.astype(jnp.bfloat16)).astype(jnp.float32)
    prob_grad = jnp.einsum('pfkgd,ptkd->pkgft', upstream, value_heads)
    score_grad = probabilities * (prob_grad - lax.optimization_barrier(jnp.sum(probabilities * prob_grad, axis=-1, keepdims=True)))
    score_low = lax.optimization_barrier(score_grad.astype(jnp.bfloat16)).astype(jnp.float32)
    value_grad = jnp.einsum('pkgft,pfkgd->ptkd', probs_low, upstream)
    key_grad = jnp.einsum('pkgft,pfkgd->ptkd', score_low, query_heads) * score_scale
    joined = jnp.concatenate([key_grad.reshape(token_count, -1), value_grad.reshape(token_count, -1)], axis=1)
    return joined.astype(jnp.bfloat16)

def reference(latent_tokens, actions, action_table, key_value_weight, queries, output_cotangent, outer_delta, momentum, anchor):

    def one_replica(member):
        latents, frame_actions, weight, query_rows, cotangent = member
        conditioned = condition(latents, frame_actions, action_table)
        key_value = jnp.dot(conditioned, weight, preferred_element_type=jnp.float32).astype(jnp.bfloat16)
        key_value_grad = attention_grad(key_value, query_rows, cotangent)
        return jnp.dot(conditioned.T, key_value_grad, preferred_element_type=jnp.float32).astype(jnp.bfloat16)
    weight_gradient = lax.map(one_replica, (latent_tokens, actions, key_value_weight, queries, output_cotangent))
    summed = lax.optimization_barrier(jnp.sum(outer_delta, axis=0))
    average = summed / N_REP
    new_momentum = MOMENTUM_RATE * momentum + average
    new_anchor = anchor - OUTER_RATE * (average + MOMENTUM_RATE * new_momentum)
    return (weight_gradient, new_momentum, new_anchor)
```

```python
import functools

import jax
import jax.numpy as jnp
from jax import lax
from jax.experimental import pallas as pl
from jax.experimental.pallas import tpu as pltpu
from jax.sharding import PartitionSpec as P

MESH = pl.DeviceIdType.MESH
HEAD_DIM = 128
KV_HEADS = 4
GROUP = 4
ACTIONS = 8
FRAMES = 16
MOMENTUM_RATE = 0.9
OUTER_RATE = 0.7

TOK = 512
BLK = 512
HW = 2 * HEAD_DIM
CH = 128
LOG2E = 1.4426950408889634


def ring_index(core, half, pos):
    even = 4 * half + pos
    row = lax.rem(lax.div(pos + 1, 2), 2)
    odd = 4 * row + half + lax.div(pos, 2) * (3 - 2 * half)
    return even + core * (odd - even)


def kernel(
    lat, w, emb, q, cot, delta, mom, anc,
    wg_out, nm_out, na_out,
    X, XT, WG, QV, CV, EM, MK, O, KS, KR, G, S3, S2, S1, T2, T1, G0, OA, OB, RL, RR, OUT,
    DL, CR, AC, R1, R2, R3, R4, FU, MO, AN, NM, NA,
    send, recv, local,
):
    f32, bf16 = jnp.float32, jnp.bfloat16
    rep = lax.axis_index("rep")
    fsdp = lax.axis_index("fsdp")
    core = lax.rem(rep, 2)
    y_hi = lax.rem(lax.div(rep, 2), 2)
    z = lax.div(rep, 4)
    hi, lo = lax.div(fsdp, 4), lax.rem(fsdp, 4)
    u = lax.div(lo, 2)
    half = hi + core * (lo + u * (3 - 2 * lo) - hi)
    pos = lo + core * (hi + u * (3 - 2 * hi) - lo)
    slot_pos = [pos, lax.rem(pos + 3, 4), lax.rem(pos + 1, 4), lax.rem(pos + 2, 4)]
    mine = [ring_index(core, half, s) for s in slot_pos]
    theirs = [ring_index(core, 1 - half, s) for s in slot_pos]
    left, right, partner = {"fsdp": mine[1]}, {"fsdp": mine[2]}, {"fsdp": theirs[0]}

    def rep_peer(z_, y_, c_):
        return {"rep": z_ * 4 + y_ * 2 + c_}

    bit1, bit2, bit4 = lax.rem(z, 2), lax.rem(lax.div(z, 2), 2), lax.div(z, 4)
    sibling = rep_peer(z, y_hi, 1 - core)
    z_one = rep_peer(z + 1 - 2 * bit1, y_hi, core)
    z_two = rep_peer(z + 2 - 4 * bit2, y_hi, core)
    z_four = rep_peer(z + 4 - 8 * bit4, y_hi, core)
    across = rep_peer(z, 1 - y_hi, core)

    counts = {"remote": 0, "local": 0}

    def remote(src, dst, device):
        n = counts["remote"]
        counts["remote"] = n + 1
        return pltpu.make_async_remote_copy(
            src_ref=src, dst_ref=dst, send_sem=send.at[n], recv_sem=recv.at[n],
            device_id=device, device_id_type=MESH,
        )

    def nearby(src, dst):
        n = counts["local"]
        counts["local"] = n + 1
        return pltpu.make_async_copy(src, dst, local.at[n])

    def columns(i):
        return pl.ds(pl.multiple_of(i * BLK, BLK), BLK)

    keys, values = pl.ds(0, HEAD_DIM), pl.ds(HEAD_DIM, HEAD_DIM)
    own, other = pl.ds(0, TOK), pl.ds(TOK, TOK)

    load_w = [
        [
            nearby(w.at[0, :, pl.ds(k * HEAD_DIM, HEAD_DIM)], WG.at[k, 0, :, keys]),
            nearby(w.at[0, :, pl.ds((KV_HEADS + k) * HEAD_DIM, HEAD_DIM)], WG.at[k, 0, :, values]),
        ]
        for k in range(KV_HEADS)
    ]
    load_x = [nearby(lat.at[0, :, columns(mine[s])], X.at[s, own, :]) for s in range(4)]
    load_emb = nearby(emb, EM)
    load_delta = nearby(delta.at[0], DL)
    load_q, load_c = nearby(q.at[0], QV), nearby(cot.at[0], CV)
    load_m, load_a = nearby(mom, MO), nearby(anc, AN)
    for c in load_w[0]:
        c.start()
    load_delta.start()
    load_emb.start()
    for c in load_x:
        c.start()
    for k in range(1, KV_HEADS):
        for c in load_w[k]:
            c.start()
    for c in (load_q, load_c, load_m, load_a):
        c.start()

    lat_send = [
        remote(lat.at[0, :, columns(theirs[s])], X.at[s, other, :], partner) for s in range(4)
    ]
    w_right = [remote(WG.at[k, 0], WG.at[k, 1], right) for k in range(KV_HEADS)]
    w_left = [remote(WG.at[k, 0], WG.at[k, 2], left) for k in range(KV_HEADS)]
    w_right2 = [remote(WG.at[k, 1, :, keys], WG.at[k, 3, :, keys], right) for k in range(KV_HEADS)]
    w_left2 = [remote(WG.at[k, 2, :, values], WG.at[k, 3, :, values], left) for k in range(KV_HEADS)]
    kv_send = [remote(KS.at[k], KR.at[k], partner) for k in range(KV_HEADS)]
    g_send = [remote(G.at[k, own, :], G.at[k, other, :], partner) for k in range(KV_HEADS)]
    opp_right = [remote(S3.at[k, :, keys], OA.at[k], right) for k in range(KV_HEADS)]
    opp_left = [remote(S3.at[k, :, values], OB.at[k], left) for k in range(KV_HEADS)]
    to_right_k = [remote(S2.at[k, :, keys], RL.at[k, :, keys], right) for k in range(KV_HEADS)]
    to_right_v = [remote(S2.at[k, :, values], RL.at[k, :, values], right) for k in range(KV_HEADS)]
    to_left_k = [remote(S1.at[k, :, keys], RR.at[k, :, keys], left) for k in range(KV_HEADS)]
    to_left_v = [remote(S1.at[k, :, values], RR.at[k, :, values], left) for k in range(KV_HEADS)]

    rows_mine = pl.ds(pl.multiple_of(core * 16, 16), 16)
    rows_other = pl.ds(pl.multiple_of((1 - core) * 16, 16), 16)

    def cols_at(start, width):
        return pl.ds(pl.multiple_of(start, 256), width)

    c1 = bit1 * 2048
    c2 = c1 + bit2 * 1024
    c4 = c2 + bit4 * 512
    cy = c4 + y_hi * 256
    o1 = (1 - bit1) * 2048
    o2 = c1 + (1 - bit2) * 1024
    o4 = c2 + (1 - bit4) * 512
    oy = c4 + (1 - y_hi) * 256
    halve = [
        remote(DL.at[rows_other, :], CR, sibling),
        remote(AC.at[:, cols_at(o1, 2048)], R1, z_one),
        remote(AC.at[:, cols_at(o2, 1024)], R2, z_two),
        remote(AC.at[:, cols_at(o4, 512)], R3, z_four),
        remote(AC.at[:, cols_at(oy, 256)], R4, across),
    ]
    double = [
        remote(FU.at[rows_mine, cols_at(s, n)], FU.at[rows_mine, cols_at(s, n)], d)
        for s, n, d in ((cy, 256, across), (c4, 512, z_four), (c2, 1024, z_two), (c1, 2048, z_one))
    ]
    double.append(remote(FU.at[rows_mine, :], FU.at[rows_mine, :], sibling))

    def outer_halve(step):
        halve[step].wait_recv()
        if step == 0:
            AC[...] = DL[rows_mine, :] + CR[...]
        else:
            start, width, got = ((c1, 2048, R1), (c2, 1024, R2), (c4, 512, R3), (cy, 256, R4))[step - 1]
            total = AC[:, cols_at(start, width)] + got[...]
            if step < 4:
                AC[:, cols_at(start, width)] = total
            else:
                FU[rows_mine, cols_at(start, width)] = total
        if step < 4:
            halve[step + 1].start()
        else:
            double[0].start()

    def outer_double(step):
        double[step].wait_recv()
        if step < 4:
            double[step + 1].start()

    store_m, store_a = nearby(NM, nm_out), nearby(NA, na_out)

    def outer_update():
        load_m.wait()
        load_a.wait()
        average = FU[...] * f32(1.0 / 32.0)
        momentum = f32(MOMENTUM_RATE) * MO[...] + average
        NM[...] = momentum
        NA[...] = AN[...] - f32(OUTER_RATE) * (average + f32(MOMENTUM_RATE) * momentum)
        store_m.start()
        store_a.start()

    def condition(s, base):
        shift = EM[:, columns(mine[s])].astype(f32)

        def chunk(i, _):
            rows = pl.ds(pl.multiple_of(base + i * 64, 64), 64)
            wide = X[s, rows, :].astype(f32).reshape(4, FRAMES, BLK) + shift[None]
            X[s, rows, :] = wide.reshape(64, BLK).astype(bf16)
            return 0

        lax.fori_loop(0, TOK // 64, chunk, 0)

    def transpose(s, base):
        def chunk(i, _):
            rows = pl.ds(pl.multiple_of(base + i * 128, 128), 128)
            XT[s, :, rows] = X[s, rows, :].T
            return 0

        lax.fori_loop(0, TOK // 128, chunk, 0)

    def project(k, rows):
        total = jnp.dot(X[0, rows, :], WG[k, 0], preferred_element_type=f32)
        for s in range(1, 4):
            total += jnp.dot(X[s, rows, :], WG[k, s], preferred_element_type=f32)
        return total

    def project_other(k):
        KS[k] = project(k, other).astype(bf16)
        kv_send[k].start()

    def project_own(k):
        O[k] = project(k, own)

    def send_w(k):
        for c in load_w[k]:
            c.wait()
        w_right[k].start()
        w_left[k].start()

    def forward_w(k):
        w_right[k].wait_recv()
        w_right2[k].start()
        w_left[k].wait_recv()
        w_left2[k].start()

    def have_w(k):
        w_right2[k].wait_recv()
        w_left2[k].wait_recv()

    def attention(k):
        kv_send[k].wait_recv()
        scale = HEAD_DIM**-0.5
        nt = (((1,), (1,)), ((), ()))

        def block(b, _):
            rows = pl.ds(pl.multiple_of(b * CH, CH), CH)
            kv = (O[k, rows, :] + KR[k, rows, :].astype(f32)).astype(bf16)
            key, value = kv[:, :HEAD_DIM], kv[:, HEAD_DIM:]
            heads = [pl.ds((k * GROUP + j) * HEAD_DIM, HEAD_DIM) for j in range(GROUP)]
            query = jnp.concatenate([QV[rows, h] for h in heads], axis=0)
            up = jnp.concatenate([CV[rows, h] for h in heads], axis=0)
            keep = MK[...] > 0.0
            scores = lax.dot_general(key, query, nt, preferred_element_type=f32)
            scores = jnp.where(keep, scores, f32(-1e30))
            top = jnp.max(scores, axis=0, keepdims=True)
            grown = jnp.exp2((scores - top) * f32(scale * LOG2E))
            probs = grown * (1.0 / jnp.sum(grown, axis=0, keepdims=True))
            prob_grad = lax.dot_general(value, up, nt, preferred_element_type=f32)
            mean = jnp.sum(probs * prob_grad, axis=0, keepdims=True)
            score_grad = (probs * (prob_grad - mean)).astype(bf16)
            G[k, rows, values] = jnp.dot(
                probs.astype(bf16), up, preferred_element_type=f32
            ).astype(bf16)
            G[k, rows, keys] = (
                jnp.dot(score_grad, query, preferred_element_type=f32) * f32(scale)
            ).astype(bf16)
            return 0

        lax.fori_loop(0, TOK // CH, block, 0)
        g_send[k].start()

    def gradient(k):
        g_send[k].wait_recv()
        S3[k] = jnp.dot(XT[3], G[k], preferred_element_type=f32).astype(bf16)
        opp_right[k].start()
        opp_left[k].start()
        to_r = jnp.dot(XT[2], G[k], preferred_element_type=f32)
        T2[k] = to_r[:, :HEAD_DIM]
        S2[k, :, values] = to_r[:, HEAD_DIM:].astype(bf16)
        to_right_v[k].start()
        to_l = jnp.dot(XT[1], G[k], preferred_element_type=f32)
        T1[k] = to_l[:, HEAD_DIM:]
        S1[k, :, keys] = to_l[:, :HEAD_DIM].astype(bf16)
        to_left_k[k].start()
        G0[k] = jnp.dot(XT[0], G[k], preferred_element_type=f32)

    def relay(k):
        opp_right[k].wait_recv()
        S2[k, :, keys] = (T2[k] + OA[k].astype(f32)).astype(bf16)
        to_right_k[k].start()
        opp_left[k].wait_recv()
        S1[k, :, values] = (T1[k] + OB[k].astype(f32)).astype(bf16)
        to_left_v[k].start()

    store_w = [
        [
            nearby(OUT.at[k, :, keys], wg_out.at[0, :, pl.ds(k * HEAD_DIM, HEAD_DIM)]),
            nearby(OUT.at[k, :, values], wg_out.at[0, :, pl.ds((KV_HEADS + k) * HEAD_DIM, HEAD_DIM)]),
        ]
        for k in range(KV_HEADS)
    ]

    def finish(k):
        for c in (to_right_k[k], to_right_v[k], to_left_k[k], to_left_v[k]):
            c.wait_recv()
        OUT[k] = (G0[k] + RL[k].astype(f32) + RR[k].astype(f32)).astype(bf16)
        for c in store_w[k]:
            c.start()

    barrier = pltpu.get_barrier_semaphore()
    peers = (partner, left, right, sibling, z_one, z_two, z_four, across)
    for peer in peers:
        pl.semaphore_signal(barrier, inc=1, device_id=peer, device_id_type=MESH)
    pl.semaphore_wait(barrier, len(peers))

    for c in lat_send:
        c.start()
    send_w(0)
    load_delta.wait()
    halve[0].start()

    t_at = lax.broadcasted_iota(jnp.int32, (CH, CH), 0)
    f_at = lax.broadcasted_iota(jnp.int32, (CH, CH), 1)
    seen = (lax.shift_right_logical(t_at, 4) == lax.shift_right_logical(f_at, 4)) & (t_at <= f_at)
    one = jnp.where(seen, f32(1.0), f32(0.0))
    for j in range(GROUP):
        MK[:, pl.ds(j * CH, CH)] = one

    load_emb.wait()
    for s in range(4):
        load_x[s].wait()
        condition(s, 0)
    outer_halve(0)
    forward_w(0)
    for s in range(4):
        transpose(s, 0)
    outer_halve(1)
    have_w(0)
    project_own(0)
    outer_halve(2)
    for s in range(4):
        lat_send[s].wait_recv()
        condition(s, TOK)
        if s == 1:
            outer_halve(3)
        if s == 2:
            send_w(1)
            outer_halve(4)
    project_other(0)
    send_w(2)
    for s in range(4):
        transpose(s, TOK)
    outer_double(0)
    forward_w(1)
    load_q.wait()
    load_c.wait()
    have_w(1)
    project_other(1)
    project_own(1)
    attention(0)
    send_w(3)
    forward_w(2)
    outer_double(1)
    have_w(2)
    project_other(2)
    project_own(2)
    attention(1)
    forward_w(3)
    gradient(0)
    outer_double(2)
    have_w(3)
    project_other(3)
    project_own(3)
    attention(2)
    gradient(1)
    relay(0)
    outer_double(3)
    attention(3)
    gradient(2)
    relay(1)
    finish(0)
    outer_double(4)
    outer_update()
    gradient(3)
    relay(2)
    finish(1)
    relay(3)
    finish(2)
    finish(3)

    for group in (
        lat_send, w_right, w_left, w_right2, w_left2, kv_send, g_send, opp_right, opp_left,
        to_right_k, to_right_v, to_left_k, to_left_v, halve, double,
    ):
        for c in group:
            c.wait_send()
    for pair in store_w:
        for c in pair:
            c.wait()
    store_m.wait()
    store_a.wait()


def body(
    latent_tokens,
    actions,
    action_table,
    key_value_weight,
    queries,
    output_cotangent,
    outer_delta,
    momentum,
    anchor,
):
    f32, bf16 = jnp.float32, jnp.bfloat16
    one_hot = (actions[0][:, None] == jnp.arange(ACTIONS, dtype=jnp.int32)[None, :]).astype(bf16)
    emb = jnp.dot(one_hot, action_table, preferred_element_type=f32).astype(bf16)
    H = KV_HEADS
    vm = pltpu.VMEM
    scratch = [
        vm((4, 2 * TOK, BLK), bf16),
        vm((4, BLK, 2 * TOK), bf16),
        vm((H, 4, BLK, HW), bf16),
        vm((TOK, 2048), bf16),
        vm((TOK, 2048), bf16),
        vm((FRAMES, 4096), bf16),
        vm((CH, GROUP * CH), f32),
        vm((H, TOK, HW), f32),
        vm((H, TOK, HW), bf16),
        vm((H, TOK, HW), bf16),
        vm((H, 2 * TOK, HW), bf16),
        vm((H, BLK, HW), bf16),
        vm((H, BLK, HW), bf16),
        vm((H, BLK, HW), bf16),
        vm((H, BLK, HEAD_DIM), f32),
        vm((H, BLK, HEAD_DIM), f32),
        vm((H, BLK, HW), f32),
        vm((H, BLK, HEAD_DIM), bf16),
        vm((H, BLK, HEAD_DIM), bf16),
        vm((H, BLK, HW), bf16),
        vm((H, BLK, HW), bf16),
        vm((H, BLK, HW), bf16),
        vm((32, 4096), f32),
        vm((16, 4096), f32),
        vm((16, 4096), f32),
        vm((16, 2048), f32),
        vm((16, 1024), f32),
        vm((16, 512), f32),
        vm((16, 256), f32),
        vm((32, 4096), f32),
        vm((32, 4096), f32),
        vm((32, 4096), f32),
        vm((32, 4096), f32),
        vm((32, 4096), f32),
        pltpu.SemaphoreType.DMA((62,)),
        pltpu.SemaphoreType.DMA((62,)),
        pltpu.SemaphoreType.DMA((32,)),
    ]
    hbm = pl.BlockSpec(memory_space=pl.ANY)
    return pl.pallas_call(
        kernel,
        out_shape=(
            jax.ShapeDtypeStruct((1, BLK, 2 * H * HEAD_DIM), bf16),
            jax.ShapeDtypeStruct((32, 4096), f32),
            jax.ShapeDtypeStruct((32, 4096), f32),
        ),
        in_specs=[hbm] * 8,
        out_specs=(hbm, hbm, hbm),
        scratch_shapes=scratch,
        compiler_params=pltpu.CompilerParams(
            collective_id=0, has_side_effects=True, vmem_limit_bytes=56 * 2**20
        ),
        cost_estimate=pl.CostEstimate(
            flops=10 * 10**9, bytes_accessed=16 * 2**20, transcendentals=10**6
        ),
    )(
        latent_tokens, key_value_weight, emb, queries, output_cotangent, outer_delta, momentum, anchor
    )


def solution(mesh):
    return jax.shard_map(
        body,
        mesh=mesh,
        in_specs=(
            P("rep", "fsdp", None),
            P("rep", None),
            P(),
            P("rep", "fsdp", None),
            P("rep", "fsdp", None),
            P("rep", "fsdp", None),
            P("rep", "fsdp", None),
            P("fsdp", None),
            P("fsdp", None),
        ),
        out_specs=(P("rep", "fsdp", None), P("fsdp", None), P("fsdp", None)),
        check_vma=False,
    )
```

```python
import functools

import jax
import jax.numpy as jnp
from jax import lax
from jax.experimental import pallas as pl
from jax.experimental.pallas import tpu as pltpu
from jax.sharding import PartitionSpec as P

MESH = pl.DeviceIdType.MESH
HEAD_DIM = 128
KV_HEADS = 4
GROUP = 4
ACTIONS = 8
FRAMES = 16
MOMENTUM_RATE = 0.9
OUTER_RATE = 0.7

TOK = 512
BLK = 512
HW = 2 * HEAD_DIM
CH = 128
VIA_B = 192
LOG2E = 1.4426950408889634


def ring_index(core, half, pos):
    even = 4 * half + pos
    row = lax.rem(lax.div(pos + 1, 2), 2)
    odd = 4 * row + half + lax.div(pos, 2) * (3 - 2 * half)
    return even + core * (odd - even)


def kernel(
    lat, act, table, w, q, cot, delta, mom, anc,
    wg_out, nm_out, na_out,
    X, XT, WG, QV, CV, TB, SA, EM, MK, O, KS, KR, G, S3, S2, S1, T2, T1, G0, OA, OB, RA, RB,
    DL, CR, AC, R1, R2, R3, R4, FU, MO, AN,
    send, recv, local,
):
    f32, bf16 = jnp.float32, jnp.bfloat16
    rep = lax.axis_index("rep")
    fsdp = lax.axis_index("fsdp")
    core = lax.rem(rep, 2)
    y_hi = lax.rem(lax.div(rep, 2), 2)
    z = lax.div(rep, 4)
    hi, lo = lax.div(fsdp, 4), lax.rem(fsdp, 4)
    u = lax.div(lo, 2)
    half = hi + core * (lo + u * (3 - 2 * lo) - hi)
    pos = lo + core * (hi + u * (3 - 2 * hi) - lo)
    odd = lax.rem(pos, 2)
    slot_pos = [pos, lax.rem(pos + 3 + 2 * odd, 4), lax.rem(pos + 1 + 2 * odd, 4), lax.rem(pos + 2, 4)]
    mine = [ring_index(core, half, s) for s in slot_pos]
    theirs = [ring_index(core, 1 - half, s) for s in slot_pos]
    to_a, to_b, partner = {"fsdp": mine[1]}, {"fsdp": mine[2]}, {"fsdp": theirs[0]}

    def rep_peer(z_, y_, c_):
        return {"rep": z_ * 4 + y_ * 2 + c_}

    bit1, bit2, bit4 = lax.rem(z, 2), lax.rem(lax.div(z, 2), 2), lax.div(z, 4)
    sibling = rep_peer(z, y_hi, 1 - core)
    z_one = rep_peer(z + 1 - 2 * bit1, y_hi, core)
    z_two = rep_peer(z + 2 - 4 * bit2, y_hi, core)
    z_four = rep_peer(z + 4 - 8 * bit4, y_hi, core)
    across = rep_peer(z, 1 - y_hi, core)

    counts = {"remote": 0, "local": 0}
    loaded = set()

    def remote(src, dst, device):
        n = counts["remote"]
        counts["remote"] = n + 1
        return pltpu.make_async_remote_copy(
            src_ref=src, dst_ref=dst, send_sem=send.at[n], recv_sem=recv.at[n],
            device_id=device, device_id_type=MESH,
        )

    def nearby(src, dst):
        n = counts["local"]
        counts["local"] = n + 1
        return pltpu.make_async_copy(src, dst, local.at[n])

    def columns(i):
        return pl.ds(pl.multiple_of(i * BLK, BLK), BLK)

    keys, values = pl.ds(0, HEAD_DIM), pl.ds(HEAD_DIM, HEAD_DIM)
    own, other = pl.ds(0, TOK), pl.ds(TOK, TOK)
    low, high = pl.ds(0, VIA_B), pl.ds(VIA_B, BLK - VIA_B)

    load_w = [
        [
            nearby(w.at[0, :, pl.ds(k * HEAD_DIM, HEAD_DIM)], WG.at[k, 0, :, keys]),
            nearby(w.at[0, :, pl.ds((KV_HEADS + k) * HEAD_DIM, HEAD_DIM)], WG.at[k, 0, :, values]),
        ]
        for k in range(KV_HEADS)
    ]
    load_x = [nearby(lat.at[0, :, columns(mine[s])], X.at[s, own, :]) for s in range(4)]
    load_act, load_table = nearby(act, SA), nearby(table, TB)
    load_delta = nearby(delta.at[0], DL)
    load_q, load_c = nearby(q.at[0], QV), nearby(cot.at[0], CV)
    load_m, load_a = nearby(mom, MO), nearby(anc, AN)
    for c in load_w[0]:
        c.start()
    load_delta.start()
    load_act.start()
    load_table.start()
    for c in load_x:
        c.start()
    for k in range(1, KV_HEADS):
        for c in load_w[k]:
            c.start()
    for c in (load_q, load_c, load_m, load_a):
        c.start()

    lat_send = [
        remote(lat.at[0, :, columns(theirs[s])], X.at[s, other, :], partner) for s in range(4)
    ]
    w_a = [remote(WG.at[k, 0], WG.at[k, 1], to_a) for k in range(KV_HEADS)]
    w_b = [remote(WG.at[k, 0], WG.at[k, 2], to_b) for k in range(KV_HEADS)]
    w_ab = [remote(WG.at[k, 1, low], WG.at[k, 3, low], to_b) for k in range(KV_HEADS)]
    w_ba = [remote(WG.at[k, 2, high], WG.at[k, 3, high], to_a) for k in range(KV_HEADS)]
    kv_send = [remote(KS.at[k], KR.at[k], partner) for k in range(KV_HEADS)]
    g_send = [remote(G.at[k, own, :], G.at[k, other, :], partner) for k in range(KV_HEADS)]
    opp_a = [remote(S3.at[k, high], OA.at[k], to_a) for k in range(KV_HEADS)]
    opp_b = [remote(S3.at[k, low], OB.at[k], to_b) for k in range(KV_HEADS)]
    sum_b_low = [remote(S2.at[k, low], RB.at[k, low], to_b) for k in range(KV_HEADS)]
    sum_b_high = [remote(S2.at[k, high], RB.at[k, high], to_b) for k in range(KV_HEADS)]
    sum_a_low = [remote(S1.at[k, low], RA.at[k, low], to_a) for k in range(KV_HEADS)]
    sum_a_high = [remote(S1.at[k, high], RA.at[k, high], to_a) for k in range(KV_HEADS)]

    rows_mine = pl.ds(pl.multiple_of(core * 16, 16), 16)
    rows_other = pl.ds(pl.multiple_of((1 - core) * 16, 16), 16)

    def cols_at(start, width):
        return pl.ds(pl.multiple_of(start, 256), width)

    c1 = bit1 * 2048
    c2 = c1 + bit2 * 1024
    c4 = c2 + bit4 * 512
    cy = c4 + y_hi * 256
    o1 = (1 - bit1) * 2048
    o2 = c1 + (1 - bit2) * 1024
    o4 = c2 + (1 - bit4) * 512
    oy = c4 + (1 - y_hi) * 256
    halve = [
        remote(DL.at[rows_other, :], CR, sibling),
        remote(AC.at[:, cols_at(o1, 2048)], R1, z_one),
        remote(AC.at[:, cols_at(o2, 1024)], R2, z_two),
        remote(AC.at[:, cols_at(o4, 512)], R3, z_four),
        remote(AC.at[:, cols_at(oy, 256)], R4, across),
    ]
    double = [
        remote(FU.at[rows_mine, cols_at(s, n)], FU.at[rows_mine, cols_at(s, n)], d)
        for s, n, d in ((cy, 256, across), (c4, 512, z_four), (c2, 1024, z_two), (c1, 2048, z_one))
    ]
    double.append(remote(FU.at[rows_mine, :], FU.at[rows_mine, :], sibling))

    def outer_halve(step):
        halve[step].wait_recv()
        if step == 0:
            AC[...] = DL[rows_mine, :] + CR[...]
        else:
            start, width, got = ((c1, 2048, R1), (c2, 1024, R2), (c4, 512, R3), (cy, 256, R4))[step - 1]
            total = AC[:, cols_at(start, width)] + got[...]
            if step < 4:
                AC[:, cols_at(start, width)] = total
            else:
                FU[rows_mine, cols_at(start, width)] = total
        if step < 4:
            halve[step + 1].start()
        else:
            double[0].start()

    def outer_double(step):
        double[step].wait_recv()
        if step < 4:
            double[step + 1].start()

    def outer_update():
        load_m.wait()
        load_a.wait()
        average = FU[...] * f32(1.0 / 32.0)
        momentum = f32(MOMENTUM_RATE) * MO[...] + average
        nm_out[...] = momentum
        na_out[...] = AN[...] - f32(OUTER_RATE) * (average + f32(MOMENTUM_RATE) * momentum)

    def build_mask():
        t_at = lax.broadcasted_iota(jnp.int32, (CH, CH), 0)
        f_at = lax.broadcasted_iota(jnp.int32, (CH, CH), 1)
        seen = (lax.shift_right_logical(t_at, 4) == lax.shift_right_logical(f_at, 4)) & (t_at <= f_at)
        one = jnp.where(seen, f32(1.0), f32(0.0))
        for j in range(GROUP):
            MK[:, pl.ds(j * CH, CH)] = one

    def embed():
        load_act.wait()
        load_table.wait()
        frame = lax.broadcasted_iota(jnp.int32, (FRAMES, BLK), 0)
        chosen = jnp.zeros((FRAMES, BLK), jnp.int32)
        for f in range(FRAMES):
            chosen = jnp.where(frame == f, SA[0, f], chosen)
        for s in range(4):
            rows = TB[:, columns(mine[s])].astype(f32)
            shift = jnp.zeros((FRAMES, BLK), f32)
            for a in range(ACTIONS):
                shift = jnp.where(chosen == a, rows[a : a + 1, :], shift)
            EM[s] = shift

    def condition(s, base):
        shift = EM[s]

        def chunk(i, _):
            rows = pl.ds(pl.multiple_of(base + i * 64, 64), 64)
            wide = X[s, rows, :].astype(f32).reshape(4, FRAMES, BLK) + shift[None]
            X[s, rows, :] = wide.reshape(64, BLK).astype(bf16)
            return 0

        lax.fori_loop(0, TOK // 64, chunk, 0)

    def transpose(s, base):
        def chunk(i, _):
            rows = pl.ds(pl.multiple_of(base + i * 128, 128), 128)
            XT[s, :, rows] = X[s, rows, :].T
            return 0

        lax.fori_loop(0, TOK // 128, chunk, 0)

    def project(k, rows):
        total = jnp.dot(X[0, rows, :], WG[k, 0], preferred_element_type=f32)
        for s in range(1, 4):
            total += jnp.dot(X[s, rows, :], WG[k, s], preferred_element_type=f32)
        return total

    def project_other(k):
        KS[k] = project(k, other).astype(bf16)
        kv_send[k].start()

    def condition_own(s):
        load_x[s].wait()
        condition(s, 0)

    def condition_other(s):
        lat_send[s].wait_recv()
        condition(s, TOK)

    def project_first(s):
        part = jnp.dot(X[s, other, :], WG[0, s], preferred_element_type=f32)
        if s == 0:
            G0[0] = part
        elif s < 3:
            G0[0] += part
        else:
            KS[0] = (G0[0] + part).astype(bf16)
            kv_send[0].start()

    def project_own(k):
        O[k] = project(k, own)

    def send_w(k, copy):
        if k not in loaded:
            loaded.add(k)
            for c in load_w[k]:
                c.wait()
        copy.start()

    def forward_ab(k):
        w_a[k].wait_recv()
        w_ab[k].start()

    def forward_ba(k):
        w_b[k].wait_recv()
        w_ba[k].start()

    def have_w(k):
        w_ab[k].wait_recv()
        w_ba[k].wait_recv()

    def attention(k):
        kv_send[k].wait_recv()
        scale = HEAD_DIM**-0.5
        nt = (((1,), (1,)), ((), ()))

        def block(b, _):
            rows = pl.ds(pl.multiple_of(b * CH, CH), CH)
            kv = (O[k, rows, :] + KR[k, rows, :].astype(f32)).astype(bf16)
            key, value = kv[:, :HEAD_DIM], kv[:, HEAD_DIM:]
            heads = [pl.ds((k * GROUP + j) * HEAD_DIM, HEAD_DIM) for j in range(GROUP)]
            query = jnp.concatenate([QV[rows, h] for h in heads], axis=0)
            up = jnp.concatenate([CV[rows, h] for h in heads], axis=0)
            keep = MK[...] > 0.0
            scores = lax.dot_general(key, query, nt, preferred_element_type=f32)
            scores = jnp.where(keep, scores, f32(-1e30))
            top = jnp.max(scores, axis=0, keepdims=True)
            grown = jnp.exp2((scores - top) * f32(scale * LOG2E))
            probs = grown * (1.0 / jnp.sum(grown, axis=0, keepdims=True))
            prob_grad = lax.dot_general(value, up, nt, preferred_element_type=f32)
            mean = jnp.sum(probs * prob_grad, axis=0, keepdims=True)
            score_grad = (probs * (prob_grad - mean)).astype(bf16)
            G[k, rows, values] = jnp.dot(
                probs.astype(bf16), up, preferred_element_type=f32
            ).astype(bf16)
            G[k, rows, keys] = (
                jnp.dot(score_grad, query, preferred_element_type=f32) * f32(scale)
            ).astype(bf16)
            return 0

        lax.fori_loop(0, TOK // CH, block, 0, unroll=4)
        g_send[k].start()

    def gradient_opposite(k):
        g_send[k].wait_recv()
        S3[k] = jnp.dot(XT[3], G[k], preferred_element_type=f32).astype(bf16)
        opp_a[k].start()
        opp_b[k].start()

    def gradient_a(k):
        part = jnp.dot(XT[1], G[k], preferred_element_type=f32)
        T1[k] = part[:VIA_B]
        S1[k, high] = part[VIA_B:].astype(bf16)
        sum_a_high[k].start()

    def gradient_b(k):
        part = jnp.dot(XT[2], G[k], preferred_element_type=f32)
        T2[k] = part[VIA_B:]
        S2[k, low] = part[:VIA_B].astype(bf16)
        sum_b_low[k].start()

    def gradient_own(k):
        G0[k] = jnp.dot(XT[0], G[k], preferred_element_type=f32)

    def relay_to_b(k):
        opp_a[k].wait_recv()
        S2[k, high] = (T2[k] + OA[k].astype(f32)).astype(bf16)
        sum_b_high[k].start()

    def relay_to_a(k):
        opp_b[k].wait_recv()
        S1[k, low] = (T1[k] + OB[k].astype(f32)).astype(bf16)
        sum_a_low[k].start()

    def finish(k):
        for c in (sum_a_low[k], sum_a_high[k], sum_b_low[k], sum_b_high[k]):
            c.wait_recv()
        total = (G0[k] + RA[k].astype(f32) + RB[k].astype(f32)).astype(bf16)
        wg_out[0, :, pl.ds(k * HEAD_DIM, HEAD_DIM)] = total[:, :HEAD_DIM]
        wg_out[0, :, pl.ds((KV_HEADS + k) * HEAD_DIM, HEAD_DIM)] = total[:, HEAD_DIM:]

    barrier = pltpu.get_barrier_semaphore()
    peers = (partner, to_a, to_b, sibling, z_one, z_two, z_four, across)
    for peer in peers:
        pl.semaphore_signal(barrier, inc=1, device_id=peer, device_id_type=MESH)
    pl.semaphore_wait(barrier, len(peers))

    lat_send[0].start()
    send_w(2, w_a[2])
    lat_send[3].start()
    send_w(1, w_a[1])
    send_w(0, w_b[0])
    load_delta.wait()
    halve[0].start()
    send_w(1, w_b[1])
    embed()
    forward_ab(2)
    condition_own(2)
    forward_ab(1)
    lat_send[2].start()
    send_w(3, w_a[3])
    send_w(0, w_a[0])
    forward_ba(1)
    outer_halve(0)
    outer_halve(1)
    outer_halve(2)
    condition_own(3)
    condition_own(1)
    lat_send[1].start()
    condition_own(0)
    have_w(1)
    condition_other(2)
    send_w(3, w_b[3])
    transpose(2, 0)
    outer_halve(3)
    transpose(3, 0)
    condition_other(3)
    forward_ab(0)
    build_mask()
    forward_ba(0)
    transpose(2, TOK)
    condition_other(0)
    outer_halve(4)
    condition_other(1)
    project_other(1)
    transpose(0, 0)
    transpose(3, TOK)
    project_own(1)
    have_w(0)
    send_w(2, w_b[2])
    transpose(0, TOK)
    forward_ab(3)
    forward_ba(3)
    load_q.wait()
    load_c.wait()
    attention(1)
    forward_ba(2)
    have_w(3)
    project_other(3)
    transpose(1, TOK)
    project_first(0)
    project_first(1)
    project_first(2)
    project_own(3)
    outer_double(0)
    transpose(1, 0)
    project_first(3)
    gradient_opposite(1)
    gradient_own(1)
    have_w(2)
    project_own(0)
    gradient_a(1)
    attention(3)
    outer_double(1)
    relay_to_a(1)
    attention(0)
    gradient_b(1)
    gradient_opposite(3)
    project_other(2)
    project_own(2)
    outer_double(2)
    gradient_a(3)
    gradient_b(3)
    outer_double(3)
    gradient_opposite(0)
    gradient_a(0)
    relay_to_b(3)
    relay_to_a(3)
    attention(2)
    relay_to_a(0)
    gradient_own(0)
    gradient_opposite(2)
    gradient_own(3)
    gradient_b(0)
    outer_double(4)
    relay_to_b(1)
    outer_update()
    relay_to_b(0)
    gradient_a(2)
    gradient_b(2)
    finish(0)
    finish(3)
    gradient_own(2)
    relay_to_b(2)
    relay_to_a(2)
    finish(1)
    finish(2)

    for group in (
        lat_send, w_a, w_b, w_ab, w_ba, kv_send, g_send, opp_a, opp_b,
        sum_a_low, sum_a_high, sum_b_low, sum_b_high, halve, double,
    ):
        for c in group:
            c.wait_send()


def body(
    latent_tokens,
    actions,
    action_table,
    key_value_weight,
    queries,
    output_cotangent,
    outer_delta,
    momentum,
    anchor,
):
    f32, bf16 = jnp.float32, jnp.bfloat16
    H = KV_HEADS
    vm = pltpu.VMEM
    scratch = [
        vm((4, 2 * TOK, BLK), bf16),
        vm((4, BLK, 2 * TOK), bf16),
        vm((H, 4, BLK, HW), bf16),
        vm((TOK, 2048), bf16),
        vm((TOK, 2048), bf16),
        vm((ACTIONS, 4096), bf16),
        pltpu.SMEM((1, FRAMES), jnp.int32),
        vm((4, FRAMES, BLK), f32),
        vm((CH, GROUP * CH), f32),
        vm((H, TOK, HW), f32),
        vm((H, TOK, HW), bf16),
        vm((H, TOK, HW), bf16),
        vm((H, 2 * TOK, HW), bf16),
        vm((H, BLK, HW), bf16),
        vm((H, BLK, HW), bf16),
        vm((H, BLK, HW), bf16),
        vm((H, BLK - VIA_B, HW), f32),
        vm((H, VIA_B, HW), f32),
        vm((H, BLK, HW), f32),
        vm((H, BLK - VIA_B, HW), bf16),
        vm((H, VIA_B, HW), bf16),
        vm((H, BLK, HW), bf16),
        vm((H, BLK, HW), bf16),
        vm((32, 4096), f32),
        vm((16, 4096), f32),
        vm((16, 4096), f32),
        vm((16, 2048), f32),
        vm((16, 1024), f32),
        vm((16, 512), f32),
        vm((16, 256), f32),
        vm((32, 4096), f32),
        vm((32, 4096), f32),
        vm((32, 4096), f32),
        pltpu.SemaphoreType.DMA((62,)),
        pltpu.SemaphoreType.DMA((62,)),
        pltpu.SemaphoreType.DMA((24,)),
    ]
    hbm = pl.BlockSpec(memory_space=pl.ANY)
    vmem = pl.BlockSpec(memory_space=pltpu.VMEM)
    return pl.pallas_call(
        kernel,
        out_shape=(
            vm((1, BLK, 2 * H * HEAD_DIM), bf16),
            vm((32, 4096), f32),
            vm((32, 4096), f32),
        ),
        in_specs=[hbm] * 9,
        out_specs=(vmem, vmem, vmem),
        scratch_shapes=scratch,
        compiler_params=pltpu.CompilerParams(
            collective_id=0, has_side_effects=True, vmem_limit_bytes=56 * 2**20
        ),
        cost_estimate=pl.CostEstimate(
            flops=10 * 10**9, bytes_accessed=16 * 2**20, transcendentals=10**6
        ),
    )(
        latent_tokens, actions, action_table, key_value_weight, queries, output_cotangent,
        outer_delta, momentum, anchor,
    )


def solution(mesh):
    return jax.shard_map(
        body,
        mesh=mesh,
        in_specs=(
            P("rep", "fsdp", None),
            P("rep", None),
            P(),
            P("rep", "fsdp", None),
            P("rep", "fsdp", None),
            P("rep", "fsdp", None),
            P("rep", "fsdp", None),
            P("fsdp", None),
            P("fsdp", None),
        ),
        out_specs=(P("rep", "fsdp", None), P("fsdp", None), P("fsdp", None)),
        check_vma=False,
    )
```

```python
import functools

import jax
import jax.numpy as jnp
from jax import lax
from jax.experimental import pallas as pl
from jax.experimental.pallas import tpu as pltpu
from jax.sharding import PartitionSpec as P

MESH = pl.DeviceIdType.MESH
HEAD_DIM = 128
KV_HEADS = 4
GROUP = 4
ACTIONS = 8
FRAMES = 16
MOMENTUM_RATE = 0.9
OUTER_RATE = 0.7

TOK = 512
BLK = 512
HW = 2 * HEAD_DIM
CH = 128
VIA_B = 336
LOG2E = 1.4426950408889634


def ring_index(core, half, pos):
    even = 4 * half + pos
    row = lax.rem(lax.div(pos + 1, 2), 2)
    odd = 4 * row + half + lax.div(pos, 2) * (3 - 2 * half)
    return even + core * (odd - even)


def kernel(
    lat, act, table, w, q, cot, delta, mom, anc,
    wg_out, nm_out, na_out,
    X, XT, WG, QV, CV, TB, SA, EM, MK, O, KS, KR, G, S3, S2, S1, T2, T1, G0, OA, OB, RA, RB,
    DL, CR, AC, R1, R2, R3, R4, FU, MO, AN,
    send, recv, local,
):
    f32, bf16 = jnp.float32, jnp.bfloat16
    rep = lax.axis_index("rep")
    fsdp = lax.axis_index("fsdp")
    core = lax.rem(rep, 2)
    y_hi = lax.rem(lax.div(rep, 2), 2)
    z = lax.div(rep, 4)
    hi, lo = lax.div(fsdp, 4), lax.rem(fsdp, 4)
    u = lax.div(lo, 2)
    half = hi + core * (lo + u * (3 - 2 * lo) - hi)
    pos = lo + core * (hi + u * (3 - 2 * hi) - lo)
    odd = lax.rem(pos, 2)
    slot_pos = [pos, lax.rem(pos + 3 + 2 * odd, 4), lax.rem(pos + 1 + 2 * odd, 4), lax.rem(pos + 2, 4)]
    mine = [ring_index(core, half, s) for s in slot_pos]
    theirs = [ring_index(core, 1 - half, s) for s in slot_pos]
    to_a, to_b, partner = {"fsdp": mine[1]}, {"fsdp": mine[2]}, {"fsdp": theirs[0]}

    def rep_peer(z_, y_, c_):
        return {"rep": z_ * 4 + y_ * 2 + c_}

    bit1, bit2, bit4 = lax.rem(z, 2), lax.rem(lax.div(z, 2), 2), lax.div(z, 4)
    sibling = rep_peer(z, y_hi, 1 - core)
    z_one = rep_peer(z + 1 - 2 * bit1, y_hi, core)
    z_two = rep_peer(z + 2 - 4 * bit2, y_hi, core)
    z_four = rep_peer(z + 4 - 8 * bit4, y_hi, core)
    across = rep_peer(z, 1 - y_hi, core)

    counts = {"remote": 0, "local": 0}
    loaded = set()

    def remote(src, dst, device):
        n = counts["remote"]
        counts["remote"] = n + 1
        return pltpu.make_async_remote_copy(
            src_ref=src, dst_ref=dst, send_sem=send.at[n], recv_sem=recv.at[n],
            device_id=device, device_id_type=MESH,
        )

    def nearby(src, dst):
        n = counts["local"]
        counts["local"] = n + 1
        return pltpu.make_async_copy(src, dst, local.at[n])

    def columns(i):
        return pl.ds(pl.multiple_of(i * BLK, BLK), BLK)

    keys, values = pl.ds(0, HEAD_DIM), pl.ds(HEAD_DIM, HEAD_DIM)
    own, other = pl.ds(0, TOK), pl.ds(TOK, TOK)
    low, high = pl.ds(0, VIA_B), pl.ds(VIA_B, BLK - VIA_B)

    load_w = [
        [
            nearby(w.at[0, :, pl.ds(k * HEAD_DIM, HEAD_DIM)], WG.at[k, 0, :, keys]),
            nearby(w.at[0, :, pl.ds((KV_HEADS + k) * HEAD_DIM, HEAD_DIM)], WG.at[k, 0, :, values]),
        ]
        for k in range(KV_HEADS)
    ]
    load_x = [nearby(lat.at[0, :, columns(mine[s])], X.at[s, own, :]) for s in range(4)]
    load_act, load_table = nearby(act, SA), nearby(table, TB)
    load_delta = nearby(delta.at[0], DL)
    load_q, load_c = nearby(q.at[0], QV), nearby(cot.at[0], CV)
    load_m, load_a = nearby(mom, MO), nearby(anc, AN)
    for c in load_w[0]:
        c.start()
    load_delta.start()
    load_act.start()
    load_table.start()
    for c in load_x:
        c.start()
    for k in range(1, KV_HEADS):
        for c in load_w[k]:
            c.start()
    for c in (load_q, load_c, load_m, load_a):
        c.start()

    lat_send = [
        remote(lat.at[0, :, columns(theirs[s])], X.at[s, other, :], partner) for s in range(4)
    ]
    w_a = [remote(WG.at[k, 0], WG.at[k, 1], to_a) for k in range(KV_HEADS)]
    w_b = [remote(WG.at[k, 0], WG.at[k, 2], to_b) for k in range(KV_HEADS)]
    w_ba = [remote(WG.at[k, 2], WG.at[k, 3], to_a) for k in range(KV_HEADS)]
    kv_send = [remote(KS.at[k], KR.at[k], partner) for k in range(KV_HEADS)]
    g_send = [remote(G.at[k, own, :], G.at[k, other, :], partner) for k in range(KV_HEADS)]
    opp_a = [remote(S3.at[k, high], OA.at[k], to_a) for k in range(KV_HEADS)]
    opp_b = [remote(S3.at[k, low], OB.at[k], to_b) for k in range(KV_HEADS)]
    sum_b_low = [remote(S2.at[k, low], RB.at[k, low], to_b) for k in range(KV_HEADS)]
    sum_b_high = [remote(S2.at[k, high], RB.at[k, high], to_b) for k in range(KV_HEADS)]
    sum_a_low = [remote(S1.at[k, low], RA.at[k, low], to_a) for k in range(KV_HEADS)]
    sum_a_high = [remote(S1.at[k, high], RA.at[k, high], to_a) for k in range(KV_HEADS)]

    rows_mine = pl.ds(pl.multiple_of(core * 16, 16), 16)
    rows_other = pl.ds(pl.multiple_of((1 - core) * 16, 16), 16)

    def cols_at(start, width):
        return pl.ds(pl.multiple_of(start, 256), width)

    c1 = bit1 * 2048
    c2 = c1 + bit2 * 1024
    c4 = c2 + bit4 * 512
    cy = c4 + y_hi * 256
    o1 = (1 - bit1) * 2048
    o2 = c1 + (1 - bit2) * 1024
    o4 = c2 + (1 - bit4) * 512
    oy = c4 + (1 - y_hi) * 256
    halve = [
        remote(DL.at[rows_other, :], CR, sibling),
        remote(AC.at[:, cols_at(o1, 2048)], R1, z_one),
        remote(AC.at[:, cols_at(o2, 1024)], R2, z_two),
        remote(AC.at[:, cols_at(o4, 512)], R3, z_four),
        remote(AC.at[:, cols_at(oy, 256)], R4, across),
    ]
    double = [
        remote(FU.at[rows_mine, cols_at(s, n)], FU.at[rows_mine, cols_at(s, n)], d)
        for s, n, d in ((cy, 256, across), (c4, 512, z_four), (c2, 1024, z_two), (c1, 2048, z_one))
    ]
    double.append(remote(FU.at[rows_mine, :], FU.at[rows_mine, :], sibling))

    bits = [None, bit1, bit2, bit4, y_hi]

    def outer_offer(step):
        @pl.when(bits[step] == 1)
        def _():
            halve[step].start()

    def outer_answer(step):
        @pl.when(bits[step] == 0)
        def _():
            halve[step].wait_recv()
            halve[step].start()

    def outer_halve(step):
        if step == 0:
            halve[0].wait_recv()
            AC[...] = DL[rows_mine, :] + CR[...]
        else:

            @pl.when(bits[step] == 1)
            def _():
                halve[step].wait_recv()

            start, width, got = ((c1, 2048, R1), (c2, 1024, R2), (c4, 512, R3), (cy, 256, R4))[step - 1]
            total = AC[:, cols_at(start, width)] + got[...]
            if step < 4:
                AC[:, cols_at(start, width)] = total
            else:
                FU[rows_mine, cols_at(start, width)] = total
        if step < 4:
            outer_offer(step + 1)
        else:
            double[0].start()

    def outer_double(step):
        double[step].wait_recv()
        if step < 4:
            double[step + 1].start()

    def outer_update():
        load_m.wait()
        load_a.wait()
        average = FU[...] * f32(1.0 / 32.0)
        momentum = f32(MOMENTUM_RATE) * MO[...] + average
        nm_out[...] = momentum
        na_out[...] = AN[...] - f32(OUTER_RATE) * (average + f32(MOMENTUM_RATE) * momentum)

    def build_mask():
        t_at = lax.broadcasted_iota(jnp.int32, (CH, CH), 0)
        f_at = lax.broadcasted_iota(jnp.int32, (CH, CH), 1)
        seen = (lax.shift_right_logical(t_at, 4) == lax.shift_right_logical(f_at, 4)) & (t_at <= f_at)
        one = jnp.where(seen, f32(1.0), f32(0.0))
        for j in range(GROUP):
            MK[:, pl.ds(j * CH, CH)] = one

    def embed():
        load_act.wait()
        load_table.wait()
        frame = lax.broadcasted_iota(jnp.int32, (FRAMES, BLK), 0)
        chosen = jnp.zeros((FRAMES, BLK), jnp.int32)
        for f in range(FRAMES):
            chosen = jnp.where(frame == f, SA[0, f], chosen)
        for s in range(4):
            rows = TB[:, columns(mine[s])].astype(f32)
            shift = jnp.zeros((FRAMES, BLK), f32)
            for a in range(ACTIONS):
                shift = jnp.where(chosen == a, rows[a : a + 1, :], shift)
            EM[s] = shift

    def condition(s, base):
        shift = EM[s]

        def chunk(i, _):
            rows = pl.ds(pl.multiple_of(base + i * 64, 64), 64)
            wide = X[s, rows, :].astype(f32).reshape(4, FRAMES, BLK) + shift[None]
            X[s, rows, :] = wide.reshape(64, BLK).astype(bf16)
            return 0

        lax.fori_loop(0, TOK // 64, chunk, 0)

    def transpose(s, base):
        def chunk(i, _):
            rows = pl.ds(pl.multiple_of(base + i * 128, 128), 128)
            XT[s, :, rows] = X[s, rows, :].T
            return 0

        lax.fori_loop(0, TOK // 128, chunk, 0)

    def project(k, rows):
        total = jnp.dot(X[0, rows, :], WG[k, 0], preferred_element_type=f32)
        for s in range(1, 4):
            total += jnp.dot(X[s, rows, :], WG[k, s], preferred_element_type=f32)
        return total

    def project_other(k):
        KS[k] = project(k, other).astype(bf16)
        kv_send[k].start()

    def condition_own(s):
        load_x[s].wait()
        condition(s, 0)

    def condition_other(s):
        lat_send[s].wait_recv()
        condition(s, TOK)

    def project_first(s):
        part = jnp.dot(X[s, other, :], WG[0, s], preferred_element_type=f32)
        if s == 0:
            G0[0] = part
        elif s < 3:
            G0[0] += part
        else:
            KS[0] = (G0[0] + part).astype(bf16)
            kv_send[0].start()

    def project_own(k):
        O[k] = project(k, own)

    def send_w(k, copy):
        if k not in loaded:
            loaded.add(k)
            for c in load_w[k]:
                c.wait()
        copy.start()

    def forward_ba(k):
        w_b[k].wait_recv()
        w_ba[k].start()

    def have_w(k):
        w_a[k].wait_recv()
        w_ba[k].wait_recv()

    def attention(k):
        kv_send[k].wait_recv()
        scale = HEAD_DIM**-0.5
        nt = (((1,), (1,)), ((), ()))

        def block(b, _):
            rows = pl.ds(pl.multiple_of(b * CH, CH), CH)
            kv = (O[k, rows, :] + KR[k, rows, :].astype(f32)).astype(bf16)
            key, value = kv[:, :HEAD_DIM], kv[:, HEAD_DIM:]
            heads = [pl.ds((k * GROUP + j) * HEAD_DIM, HEAD_DIM) for j in range(GROUP)]
            query = jnp.concatenate([QV[rows, h] for h in heads], axis=0)
            up = jnp.concatenate([CV[rows, h] for h in heads], axis=0)
            keep = MK[...] > 0.0
            scores = lax.dot_general(key, query, nt, preferred_element_type=f32)
            scores = jnp.where(keep, scores, f32(-1e30))
            top = jnp.max(scores, axis=0, keepdims=True)
            grown = jnp.exp2((scores - top) * f32(scale * LOG2E))
            probs = grown * (1.0 / jnp.sum(grown, axis=0, keepdims=True))
            prob_grad = lax.dot_general(value, up, nt, preferred_element_type=f32)
            mean = jnp.sum(probs * prob_grad, axis=0, keepdims=True)
            score_grad = (probs * (prob_grad - mean)).astype(bf16)
            G[k, rows, values] = jnp.dot(
                probs.astype(bf16), up, preferred_element_type=f32
            ).astype(bf16)
            G[k, rows, keys] = (
                jnp.dot(score_grad, query, preferred_element_type=f32) * f32(scale)
            ).astype(bf16)
            return 0

        lax.fori_loop(0, TOK // CH, block, 0, unroll=4)
        g_send[k].start()

    def gradient_opposite(k):
        g_send[k].wait_recv()
        S3[k] = jnp.dot(XT[3], G[k], preferred_element_type=f32).astype(bf16)
        opp_a[k].start()
        opp_b[k].start()

    def gradient_a(k):
        part = jnp.dot(XT[1], G[k], preferred_element_type=f32)
        T1[k] = part[:VIA_B]
        S1[k, high] = part[VIA_B:].astype(bf16)
        sum_a_high[k].start()

    def gradient_b(k):
        part = jnp.dot(XT[2], G[k], preferred_element_type=f32)
        T2[k] = part[VIA_B:]
        S2[k, low] = part[:VIA_B].astype(bf16)
        sum_b_low[k].start()

    def gradient_own(k):
        G0[k] = jnp.dot(XT[0], G[k], preferred_element_type=f32)

    def relay_to_b(k):
        opp_a[k].wait_recv()
        S2[k, high] = (T2[k] + OA[k].astype(f32)).astype(bf16)
        sum_b_high[k].start()

    def relay_to_a(k):
        opp_b[k].wait_recv()
        S1[k, low] = (T1[k] + OB[k].astype(f32)).astype(bf16)
        sum_a_low[k].start()

    def finish(k):
        for c in (sum_a_low[k], sum_a_high[k], sum_b_low[k], sum_b_high[k]):
            c.wait_recv()
        total = (G0[k] + RA[k].astype(f32) + RB[k].astype(f32)).astype(bf16)
        wg_out[0, :, pl.ds(k * HEAD_DIM, HEAD_DIM)] = total[:, :HEAD_DIM]
        wg_out[0, :, pl.ds((KV_HEADS + k) * HEAD_DIM, HEAD_DIM)] = total[:, HEAD_DIM:]

    barrier = pltpu.get_barrier_semaphore()
    peers = (partner, to_a, to_b, sibling)
    for peer in peers:
        pl.semaphore_signal(barrier, inc=1, device_id=peer, device_id_type=MESH)
    for bit, peer in ((bit1, z_one), (bit2, z_two), (bit4, z_four), (y_hi, across)):

        @pl.when(bit == 0)
        def _():
            pl.semaphore_signal(barrier, inc=1, device_id=peer, device_id_type=MESH)

    pl.semaphore_wait(barrier, len(peers) + bit1 + bit2 + bit4 + y_hi)

    send_w(1, w_b[1])
    send_w(1, w_a[1])
    embed()
    lat_send[3].start()
    send_w(2, w_a[2])
    load_delta.wait()
    halve[0].start()
    outer_halve(0)
    lat_send[0].start()
    build_mask()
    lat_send[1].start()
    outer_answer(1)
    send_w(2, w_b[2])
    forward_ba(1)
    outer_halve(1)
    condition_own(3)
    lat_send[2].start()
    outer_answer(2)
    condition_own(0)
    send_w(3, w_a[3])
    forward_ba(2)
    outer_halve(2)
    outer_answer(3)
    condition_own(2)
    send_w(0, w_b[0])
    condition_own(1)
    transpose(1, 0)
    send_w(0, w_a[0])
    send_w(3, w_b[3])
    have_w(1)
    transpose(0, 0)
    condition_other(3)
    condition_other(1)
    outer_halve(3)
    transpose(2, 0)
    condition_other(2)
    condition_other(0)
    have_w(2)
    project_own(2)
    transpose(3, TOK)
    project_other(2)
    outer_answer(4)
    forward_ba(0)
    project_own(1)
    project_other(1)
    load_q.wait()
    load_c.wait()
    attention(2)
    forward_ba(3)
    transpose(3, 0)
    outer_halve(4)
    have_w(0)
    project_first(0)
    attention(1)
    project_first(1)
    gradient_opposite(2)
    transpose(1, TOK)
    project_first(2)
    project_first(3)
    gradient_a(2)
    project_own(0)
    have_w(3)
    project_other(3)
    gradient_opposite(1)
    project_own(3)
    transpose(2, TOK)
    gradient_a(1)
    relay_to_a(2)
    outer_double(0)
    attention(0)
    transpose(0, TOK)
    relay_to_a(1)
    attention(3)
    gradient_opposite(0)
    gradient_b(2)
    outer_double(1)
    gradient_a(0)
    gradient_own(0)
    gradient_opposite(3)
    gradient_a(3)
    gradient_b(0)
    relay_to_b(2)
    gradient_b(3)
    outer_double(2)
    gradient_own(2)
    relay_to_a(0)
    relay_to_a(3)
    relay_to_b(0)
    gradient_b(1)
    gradient_own(3)
    relay_to_b(1)
    outer_double(3)
    finish(2)
    outer_double(4)
    outer_update()
    finish(0)
    gradient_own(1)
    relay_to_b(3)
    finish(1)
    finish(3)

    for group in (
        lat_send, w_a, w_b, w_ba, kv_send, g_send, opp_a, opp_b,
        sum_a_low, sum_a_high, sum_b_low, sum_b_high, halve, double,
    ):
        for c in group:
            c.wait_send()


def body(
    latent_tokens,
    actions,
    action_table,
    key_value_weight,
    queries,
    output_cotangent,
    outer_delta,
    momentum,
    anchor,
):
    f32, bf16 = jnp.float32, jnp.bfloat16
    H = KV_HEADS
    vm = pltpu.VMEM
    scratch = [
        vm((4, 2 * TOK, BLK), bf16),
        vm((4, BLK, 2 * TOK), bf16),
        vm((H, 4, BLK, HW), bf16),
        vm((TOK, 2048), bf16),
        vm((TOK, 2048), bf16),
        vm((ACTIONS, 4096), bf16),
        pltpu.SMEM((1, FRAMES), jnp.int32),
        vm((4, FRAMES, BLK), f32),
        vm((CH, GROUP * CH), f32),
        vm((H, TOK, HW), f32),
        vm((H, TOK, HW), bf16),
        vm((H, TOK, HW), bf16),
        vm((H, 2 * TOK, HW), bf16),
        vm((H, BLK, HW), bf16),
        vm((H, BLK, HW), bf16),
        vm((H, BLK, HW), bf16),
        vm((H, BLK - VIA_B, HW), f32),
        vm((H, VIA_B, HW), f32),
        vm((H, BLK, HW), f32),
        vm((H, BLK - VIA_B, HW), bf16),
        vm((H, VIA_B, HW), bf16),
        vm((H, BLK, HW), bf16),
        vm((H, BLK, HW), bf16),
        vm((32, 4096), f32),
        vm((16, 4096), f32),
        vm((16, 4096), f32),
        vm((16, 2048), f32),
        vm((16, 1024), f32),
        vm((16, 512), f32),
        vm((16, 256), f32),
        vm((32, 4096), f32),
        vm((32, 4096), f32),
        vm((32, 4096), f32),
        pltpu.SemaphoreType.DMA((58,)),
        pltpu.SemaphoreType.DMA((58,)),
        pltpu.SemaphoreType.DMA((24,)),
    ]
    hbm = pl.BlockSpec(memory_space=pl.ANY)
    vmem = pl.BlockSpec(memory_space=pltpu.VMEM)
    return pl.pallas_call(
        kernel,
        out_shape=(
            vm((1, BLK, 2 * H * HEAD_DIM), bf16),
            vm((32, 4096), f32),
            vm((32, 4096), f32),
        ),
        in_specs=[hbm] * 9,
        out_specs=(vmem, vmem, vmem),
        scratch_shapes=scratch,
        compiler_params=pltpu.CompilerParams(
            collective_id=0, has_side_effects=True, vmem_limit_bytes=56 * 2**20
        ),
        cost_estimate=pl.CostEstimate(
            flops=10 * 10**9, bytes_accessed=16 * 2**20, transcendentals=10**6
        ),
    )(
        latent_tokens, actions, action_table, key_value_weight, queries, output_cotangent,
        outer_delta, momentum, anchor,
    )


def solution(mesh):
    return jax.shard_map(
        body,
        mesh=mesh,
        in_specs=(
            P("rep", "fsdp", None),
            P("rep", None),
            P(),
            P("rep", "fsdp", None),
            P("rep", "fsdp", None),
            P("rep", "fsdp", None),
            P("rep", "fsdp", None),
            P("fsdp", None),
            P("fsdp", None),
        ),
        out_specs=(P("rep", "fsdp", None), P("fsdp", None), P("fsdp", None)),
        check_vma=False,
    )
```

```python
import functools

import jax
import jax.numpy as jnp
from jax import lax
from jax.experimental import pallas as pl
from jax.experimental.pallas import tpu as pltpu
from jax.sharding import PartitionSpec as P

MESH = pl.DeviceIdType.MESH
HEAD_DIM = 128
KV_HEADS = 4
GROUP = 4
ACTIONS = 8
FRAMES = 16
MOMENTUM_RATE = 0.9
OUTER_RATE = 0.7

TOK = 512
BLK = 512
HW = 2 * HEAD_DIM
CH = 128
VIA_B = 336
LOG2E = 1.4426950408889634


def ring_index(core, half, pos):
    even = 4 * half + pos
    row = lax.rem(lax.div(pos + 1, 2), 2)
    odd = 4 * row + half + lax.div(pos, 2) * (3 - 2 * half)
    return even + core * (odd - even)


def kernel(
    lat, act, table, w, q, cot, delta, mom, anc,
    wg_out, nm_out, na_out,
    X, XT, WG, QV, CV, TB, SA, EM, MK, O, KS, KR, G, S3, S2, S1, T2, T1, G0, OA, OB, RA, RB,
    DL, CR, AC, R1, R2, R3, R4, FU, MO, AN,
    send, recv, local,
):
    f32, bf16 = jnp.float32, jnp.bfloat16
    rep = lax.axis_index("rep")
    fsdp = lax.axis_index("fsdp")
    core = lax.rem(rep, 2)
    y_hi = lax.rem(lax.div(rep, 2), 2)
    z = lax.div(rep, 4)
    hi, lo = lax.div(fsdp, 4), lax.rem(fsdp, 4)
    u = lax.div(lo, 2)
    half = hi + core * (lo + u * (3 - 2 * lo) - hi)
    pos = lo + core * (hi + u * (3 - 2 * hi) - lo)
    odd = lax.rem(pos, 2)
    slot_pos = [pos, lax.rem(pos + 3 + 2 * odd, 4), lax.rem(pos + 1 + 2 * odd, 4), lax.rem(pos + 2, 4)]
    mine = [ring_index(core, half, s) for s in slot_pos]
    theirs = [ring_index(core, 1 - half, s) for s in slot_pos]
    to_a, to_b, partner = {"fsdp": mine[1]}, {"fsdp": mine[2]}, {"fsdp": theirs[0]}

    def rep_peer(z_, y_, c_):
        return {"rep": z_ * 4 + y_ * 2 + c_}

    bit1, bit2, bit4 = lax.rem(z, 2), lax.rem(lax.div(z, 2), 2), lax.div(z, 4)
    sibling = rep_peer(z, y_hi, 1 - core)
    z_one = rep_peer(z + 1 - 2 * bit1, y_hi, core)
    z_two = rep_peer(z + 2 - 4 * bit2, y_hi, core)
    z_four = rep_peer(z + 4 - 8 * bit4, y_hi, core)
    across = rep_peer(z, 1 - y_hi, core)

    counts = {"remote": 0, "local": 0}
    loaded = set()

    def remote(src, dst, device):
        n = counts["remote"]
        counts["remote"] = n + 1
        return pltpu.make_async_remote_copy(
            src_ref=src, dst_ref=dst, send_sem=send.at[n], recv_sem=recv.at[n],
            device_id=device, device_id_type=MESH,
        )

    def nearby(src, dst):
        n = counts["local"]
        counts["local"] = n + 1
        return pltpu.make_async_copy(src, dst, local.at[n])

    def columns(i):
        return pl.ds(pl.multiple_of(i * BLK, BLK), BLK)

    keys, values = pl.ds(0, HEAD_DIM), pl.ds(HEAD_DIM, HEAD_DIM)
    own, other = pl.ds(0, TOK), pl.ds(TOK, TOK)
    low, high = pl.ds(0, VIA_B), pl.ds(VIA_B, BLK - VIA_B)

    load_w = [
        [
            nearby(w.at[0, :, pl.ds(k * HEAD_DIM, HEAD_DIM)], WG.at[k, 0, :, keys]),
            nearby(w.at[0, :, pl.ds((KV_HEADS + k) * HEAD_DIM, HEAD_DIM)], WG.at[k, 0, :, values]),
        ]
        for k in range(KV_HEADS)
    ]
    load_x = [nearby(lat.at[0, :, columns(mine[s])], X.at[s, own, :]) for s in range(4)]
    load_act, load_table = nearby(act, SA), nearby(table, TB)
    load_delta = nearby(delta.at[0], DL)
    load_q, load_c = nearby(q.at[0], QV), nearby(cot.at[0], CV)
    load_m, load_a = nearby(mom, MO), nearby(anc, AN)
    for k in (1, 2):
        for c in load_w[k]:
            c.start()
    load_delta.start()
    load_act.start()
    load_table.start()

    lat_send = [
        remote(lat.at[0, :, columns(theirs[s])], X.at[s, other, :], partner) for s in range(4)
    ]
    w_a = [remote(WG.at[k, 0], WG.at[k, 1], to_a) for k in range(KV_HEADS)]
    w_b = [remote(WG.at[k, 0], WG.at[k, 2], to_b) for k in range(KV_HEADS)]
    w_ba = [remote(WG.at[k, 2], WG.at[k, 3], to_a) for k in range(KV_HEADS)]
    kv_send = [remote(KS.at[k], KR.at[k], partner) for k in range(KV_HEADS)]
    g_send = [remote(G.at[k, own, :], G.at[k, other, :], partner) for k in range(KV_HEADS)]
    opp_a = [remote(S3.at[k, high], OA.at[k], to_a) for k in range(KV_HEADS)]
    opp_b = [remote(S3.at[k, low], OB.at[k], to_b) for k in range(KV_HEADS)]
    sum_b_low = [remote(S2.at[k, low], RB.at[k, low], to_b) for k in range(KV_HEADS)]
    sum_b_high = [remote(S2.at[k, high], RB.at[k, high], to_b) for k in range(KV_HEADS)]
    sum_a_low = [remote(S1.at[k, low], RA.at[k, low], to_a) for k in range(KV_HEADS)]
    sum_a_high = [remote(S1.at[k, high], RA.at[k, high], to_a) for k in range(KV_HEADS)]

    rows_mine = pl.ds(pl.multiple_of(core * 16, 16), 16)
    rows_other = pl.ds(pl.multiple_of((1 - core) * 16, 16), 16)

    def cols_at(start, width):
        return pl.ds(pl.multiple_of(start, 256), width)

    c1 = bit1 * 2048
    c2 = c1 + bit2 * 1024
    c4 = c2 + bit4 * 512
    cy = c4 + y_hi * 256
    o1 = (1 - bit1) * 2048
    o2 = c1 + (1 - bit2) * 1024
    o4 = c2 + (1 - bit4) * 512
    oy = c4 + (1 - y_hi) * 256
    halve = [
        remote(DL.at[rows_other, :], CR, sibling),
        remote(AC.at[:, cols_at(o1, 2048)], R1, z_one),
        remote(AC.at[:, cols_at(o2, 1024)], R2, z_two),
        remote(AC.at[:, cols_at(o4, 512)], R3, z_four),
        remote(AC.at[:, cols_at(oy, 256)], R4, across),
    ]
    double = [
        remote(FU.at[rows_mine, cols_at(s, n)], FU.at[rows_mine, cols_at(s, n)], d)
        for s, n, d in ((cy, 256, across), (c4, 512, z_four), (c2, 1024, z_two), (c1, 2048, z_one))
    ]
    double.append(remote(FU.at[rows_mine, :], FU.at[rows_mine, :], sibling))

    bits = [None, bit1, bit2, bit4, y_hi]

    def outer_offer(step):
        @pl.when(bits[step] == 1)
        def _():
            halve[step].start()

    def outer_answer(step):
        @pl.when(bits[step] == 0)
        def _():
            halve[step].wait_recv()
            halve[step].start()

    def outer_halve(step):
        if step == 0:
            halve[0].wait_recv()
            AC[...] = DL[rows_mine, :] + CR[...]
        else:

            @pl.when(bits[step] == 1)
            def _():
                halve[step].wait_recv()

            start, width, got = ((c1, 2048, R1), (c2, 1024, R2), (c4, 512, R3), (cy, 256, R4))[step - 1]
            total = AC[:, cols_at(start, width)] + got[...]
            if step < 4:
                AC[:, cols_at(start, width)] = total
            else:
                FU[rows_mine, cols_at(start, width)] = total
        if step < 4:
            outer_offer(step + 1)
        else:
            double[0].start()

    def outer_double(step):
        double[step].wait_recv()
        if step < 4:
            double[step + 1].start()

    def outer_update():
        load_m.wait()
        load_a.wait()
        average = FU[...] * f32(1.0 / 32.0)
        momentum = f32(MOMENTUM_RATE) * MO[...] + average
        nm_out[...] = momentum
        na_out[...] = AN[...] - f32(OUTER_RATE) * (average + f32(MOMENTUM_RATE) * momentum)

    def build_mask():
        t_at = lax.broadcasted_iota(jnp.int32, (CH, CH), 0)
        f_at = lax.broadcasted_iota(jnp.int32, (CH, CH), 1)
        seen = (lax.shift_right_logical(t_at, 4) == lax.shift_right_logical(f_at, 4)) & (t_at <= f_at)
        one = jnp.where(seen, f32(1.0), f32(0.0))
        for j in range(GROUP):
            MK[:, pl.ds(j * CH, CH)] = one

    def embed():
        load_act.wait()
        load_table.wait()
        frame = lax.broadcasted_iota(jnp.int32, (FRAMES, BLK), 0)
        chosen = jnp.zeros((FRAMES, BLK), jnp.int32)
        for f in range(FRAMES):
            chosen = jnp.where(frame == f, SA[0, f], chosen)
        for s in range(4):
            rows = TB[:, columns(mine[s])].astype(f32)
            shift = jnp.zeros((FRAMES, BLK), f32)
            for a in range(ACTIONS):
                shift = jnp.where(chosen == a, rows[a : a + 1, :], shift)
            EM[s] = shift

    def condition(s, base):
        shift = EM[s]

        def chunk(i, _):
            rows = pl.ds(pl.multiple_of(base + i * 64, 64), 64)
            wide = X[s, rows, :].astype(f32).reshape(4, FRAMES, BLK) + shift[None]
            X[s, rows, :] = wide.reshape(64, BLK).astype(bf16)
            return 0

        lax.fori_loop(0, TOK // 64, chunk, 0)

    def transpose(s, base):
        def chunk(i, _):
            rows = pl.ds(pl.multiple_of(base + i * 128, 128), 128)
            XT[s, :, rows] = X[s, rows, :].T
            return 0

        lax.fori_loop(0, TOK // 128, chunk, 0)

    def project(k, rows):
        total = jnp.dot(X[0, rows, :], WG[k, 0], preferred_element_type=f32)
        for s in range(1, 4):
            total += jnp.dot(X[s, rows, :], WG[k, s], preferred_element_type=f32)
        return total

    def project_other(k):
        KS[k] = project(k, other).astype(bf16)
        kv_send[k].start()

    def condition_own(s):
        load_x[s].wait()
        condition(s, 0)

    def condition_other(s):
        lat_send[s].wait_recv()
        condition(s, TOK)

    def project_first(s):
        part = jnp.dot(X[s, other, :], WG[0, s], preferred_element_type=f32)
        if s == 0:
            G0[0] = part
        elif s < 3:
            G0[0] += part
        else:
            KS[0] = (G0[0] + part).astype(bf16)
            kv_send[0].start()

    def project_own(k):
        O[k] = project(k, own)

    def send_w(k, copy):
        if k not in loaded:
            loaded.add(k)
            for c in load_w[k]:
                c.wait()
        copy.start()

    def forward_ba(k):
        w_b[k].wait_recv()
        w_ba[k].start()

    def have_w(k):
        w_a[k].wait_recv()
        w_ba[k].wait_recv()

    def attention(k):
        kv_send[k].wait_recv()
        scale = HEAD_DIM**-0.5
        nt = (((1,), (1,)), ((), ()))

        def block(b, _):
            rows = pl.ds(pl.multiple_of(b * CH, CH), CH)
            kv = (O[k, rows, :] + KR[k, rows, :].astype(f32)).astype(bf16)
            key, value = kv[:, :HEAD_DIM], kv[:, HEAD_DIM:]
            heads = [pl.ds((k * GROUP + j) * HEAD_DIM, HEAD_DIM) for j in range(GROUP)]
            query = jnp.concatenate([QV[rows, h] for h in heads], axis=0)
            up = jnp.concatenate([CV[rows, h] for h in heads], axis=0)
            keep = MK[...] > 0.0
            scores = lax.dot_general(key, query, nt, preferred_element_type=f32)
            scores = jnp.where(keep, scores, f32(-1e30))
            top = jnp.max(scores, axis=0, keepdims=True)
            grown = jnp.exp2((scores - top) * f32(scale * LOG2E))
            probs = grown * (1.0 / jnp.sum(grown, axis=0, keepdims=True))
            prob_grad = lax.dot_general(value, up, nt, preferred_element_type=f32)
            mean = jnp.sum(probs * prob_grad, axis=0, keepdims=True)
            score_grad = (probs * (prob_grad - mean)).astype(bf16)
            G[k, rows, values] = jnp.dot(
                probs.astype(bf16), up, preferred_element_type=f32
            ).astype(bf16)
            G[k, rows, keys] = (
                jnp.dot(score_grad, query, preferred_element_type=f32) * f32(scale)
            ).astype(bf16)
            return 0

        lax.fori_loop(0, TOK // CH, block, 0, unroll=4)
        g_send[k].start()

    def gradient_opposite(k):
        g_send[k].wait_recv()
        S3[k] = jnp.dot(XT[3], G[k], preferred_element_type=f32).astype(bf16)
        opp_a[k].start()
        opp_b[k].start()

    def gradient_a(k):
        part = jnp.dot(XT[1], G[k], preferred_element_type=f32)
        T1[k] = part[:VIA_B]
        S1[k, high] = part[VIA_B:].astype(bf16)
        sum_a_high[k].start()

    def gradient_b(k):
        part = jnp.dot(XT[2], G[k], preferred_element_type=f32)
        T2[k] = part[VIA_B:]
        S2[k, low] = part[:VIA_B].astype(bf16)
        sum_b_low[k].start()

    def gradient_own(k):
        G0[k] = jnp.dot(XT[0], G[k], preferred_element_type=f32)

    def relay_to_b(k):
        opp_a[k].wait_recv()
        S2[k, high] = (T2[k] + OA[k].astype(f32)).astype(bf16)
        sum_b_high[k].start()

    def relay_to_a(k):
        opp_b[k].wait_recv()
        S1[k, low] = (T1[k] + OB[k].astype(f32)).astype(bf16)
        sum_a_low[k].start()

    def finish(k):
        for c in (sum_a_low[k], sum_a_high[k], sum_b_low[k], sum_b_high[k]):
            c.wait_recv()
        total = (G0[k] + RA[k].astype(f32) + RB[k].astype(f32)).astype(bf16)
        wg_out[0, :, pl.ds(k * HEAD_DIM, HEAD_DIM)] = total[:, :HEAD_DIM]
        wg_out[0, :, pl.ds((KV_HEADS + k) * HEAD_DIM, HEAD_DIM)] = total[:, HEAD_DIM:]

    barrier = pltpu.get_barrier_semaphore()
    peers = (partner, to_a, to_b, sibling)
    for peer in peers:
        pl.semaphore_signal(barrier, inc=1, device_id=peer, device_id_type=MESH)
    for bit, peer in ((bit1, z_one), (bit2, z_two), (bit4, z_four), (y_hi, across)):

        @pl.when(bit == 0)
        def _():
            pl.semaphore_signal(barrier, inc=1, device_id=peer, device_id_type=MESH)

    pl.semaphore_wait(barrier, len(peers) + bit1 + bit2 + bit4 + y_hi)

    send_w(1, w_b[1])
    send_w(1, w_a[1])
    embed()
    lat_send[3].start()
    send_w(2, w_a[2])
    load_delta.wait()
    halve[0].start()
    for c in load_x:
        c.start()
    for k in (0, 3):
        for c in load_w[k]:
            c.start()
    outer_halve(0)
    lat_send[0].start()
    build_mask()
    lat_send[1].start()
    outer_answer(1)
    send_w(2, w_b[2])
    forward_ba(1)
    for c in (load_q, load_c):
        c.start()
    outer_halve(1)
    condition_own(3)
    lat_send[2].start()
    outer_answer(2)
    condition_own(0)
    send_w(3, w_a[3])
    forward_ba(2)
    for c in (load_m, load_a):
        c.start()
    outer_halve(2)
    outer_answer(3)
    condition_own(2)
    send_w(0, w_b[0])
    condition_own(1)
    transpose(1, 0)
    send_w(0, w_a[0])
    send_w(3, w_b[3])
    have_w(1)
    transpose(0, 0)
    condition_other(3)
    condition_other(1)
    outer_halve(3)
    transpose(2, 0)
    condition_other(2)
    condition_other(0)
    have_w(2)
    project_own(2)
    transpose(3, TOK)
    project_other(2)
    outer_answer(4)
    forward_ba(0)
    project_own(1)
    project_other(1)
    load_q.wait()
    load_c.wait()
    attention(2)
    forward_ba(3)
    transpose(3, 0)
    outer_halve(4)
    have_w(0)
    project_first(0)
    attention(1)
    project_first(1)
    gradient_opposite(2)
    transpose(1, TOK)
    project_first(2)
    project_first(3)
    gradient_a(2)
    project_own(0)
    have_w(3)
    project_other(3)
    gradient_opposite(1)
    project_own(3)
    transpose(2, TOK)
    gradient_a(1)
    relay_to_a(2)
    outer_double(0)
    attention(0)
    transpose(0, TOK)
    relay_to_a(1)
    attention(3)
    gradient_opposite(0)
    gradient_b(2)
    outer_double(1)
    gradient_a(0)
    gradient_own(0)
    gradient_opposite(3)
    gradient_a(3)
    gradient_b(0)
    relay_to_b(2)
    gradient_b(3)
    outer_double(2)
    gradient_own(2)
    relay_to_a(0)
    relay_to_a(3)
    relay_to_b(0)
    gradient_b(1)
    gradient_own(3)
    relay_to_b(1)
    outer_double(3)
    finish(2)
    outer_double(4)
    outer_update()
    finish(0)
    gradient_own(1)
    relay_to_b(3)
    finish(1)
    finish(3)

    for group in (
        lat_send, w_a, w_b, w_ba, kv_send, g_send, opp_a, opp_b,
        sum_a_low, sum_a_high, sum_b_low, sum_b_high, halve, double,
    ):
        for c in group:
            c.wait_send()


def body(
    latent_tokens,
    actions,
    action_table,
    key_value_weight,
    queries,
    output_cotangent,
    outer_delta,
    momentum,
    anchor,
):
    f32, bf16 = jnp.float32, jnp.bfloat16
    H = KV_HEADS
    vm = pltpu.VMEM
    scratch = [
        vm((4, 2 * TOK, BLK), bf16),
        vm((4, BLK, 2 * TOK), bf16),
        vm((H, 4, BLK, HW), bf16),
        vm((TOK, 2048), bf16),
        vm((TOK, 2048), bf16),
        vm((ACTIONS, 4096), bf16),
        pltpu.SMEM((1, FRAMES), jnp.int32),
        vm((4, FRAMES, BLK), f32),
        vm((CH, GROUP * CH), f32),
        vm((H, TOK, HW), f32),
        vm((H, TOK, HW), bf16),
        vm((H, TOK, HW), bf16),
        vm((H, 2 * TOK, HW), bf16),
        vm((H, BLK, HW), bf16),
        vm((H, BLK, HW), bf16),
        vm((H, BLK, HW), bf16),
        vm((H, BLK - VIA_B, HW), f32),
        vm((H, VIA_B, HW), f32),
        vm((H, BLK, HW), f32),
        vm((H, BLK - VIA_B, HW), bf16),
        vm((H, VIA_B, HW), bf16),
        vm((H, BLK, HW), bf16),
        vm((H, BLK, HW), bf16),
        vm((32, 4096), f32),
        vm((16, 4096), f32),
        vm((16, 4096), f32),
        vm((16, 2048), f32),
        vm((16, 1024), f32),
        vm((16, 512), f32),
        vm((16, 256), f32),
        vm((32, 4096), f32),
        vm((32, 4096), f32),
        vm((32, 4096), f32),
        pltpu.SemaphoreType.DMA((58,)),
        pltpu.SemaphoreType.DMA((58,)),
        pltpu.SemaphoreType.DMA((24,)),
    ]
    hbm = pl.BlockSpec(memory_space=pl.ANY)
    vmem = pl.BlockSpec(memory_space=pltpu.VMEM)
    return pl.pallas_call(
        kernel,
        out_shape=(
            vm((1, BLK, 2 * H * HEAD_DIM), bf16),
            vm((32, 4096), f32),
            vm((32, 4096), f32),
        ),
        in_specs=[hbm] * 9,
        out_specs=(vmem, vmem, vmem),
        scratch_shapes=scratch,
        compiler_params=pltpu.CompilerParams(
            collective_id=0, has_side_effects=True, vmem_limit_bytes=56 * 2**20
        ),
        cost_estimate=pl.CostEstimate(
            flops=10 * 10**9, bytes_accessed=16 * 2**20, transcendentals=10**6
        ),
    )(
        latent_tokens, actions, action_table, key_value_weight, queries, output_cotangent,
        outer_delta, momentum, anchor,
    )


def solution(mesh):
    return jax.shard_map(
        body,
        mesh=mesh,
        in_specs=(
            P("rep", "fsdp", None),
            P("rep", None),
            P(),
            P("rep", "fsdp", None),
            P("rep", "fsdp", None),
            P("rep", "fsdp", None),
            P("rep", "fsdp", None),
            P("fsdp", None),
            P("fsdp", None),
        ),
        out_specs=(P("rep", "fsdp", None), P("fsdp", None), P("fsdp", None)),
        check_vma=False,
    )
```

```python
import functools

import jax
import jax.numpy as jnp
from jax import lax
from jax.experimental import pallas as pl
from jax.experimental.pallas import tpu as pltpu
from jax.sharding import PartitionSpec as P

MESH = pl.DeviceIdType.MESH
HEAD_DIM = 128
KV_HEADS = 4
GROUP = 4
ACTIONS = 8
FRAMES = 16
MOMENTUM_RATE = 0.9
OUTER_RATE = 0.7

TOK = 512
BLK = 512
HW = 2 * HEAD_DIM
CH = 128
VIA_B = 336
LOG2E = 1.4426950408889634


def ring_index(core, half, pos):
    even = 4 * half + pos
    row = lax.rem(lax.div(pos + 1, 2), 2)
    odd = 4 * row + half + lax.div(pos, 2) * (3 - 2 * half)
    return even + core * (odd - even)


def kernel(
    lat, act, table, w, q, cot, delta, mom, anc,
    wg_out, nm_out, na_out,
    X, XT, WG, QV, CV, TB, SA, EM, MK, O, KS, KR, G, S3, S2, S1, T2, T1, G0, OA, OB, RA, RB,
    DL, CR, AC, R1, R2, R3, R4, FU, MO, AN,
    send, recv, local,
):
    f32, bf16 = jnp.float32, jnp.bfloat16
    rep = lax.axis_index("rep")
    fsdp = lax.axis_index("fsdp")
    core = lax.rem(rep, 2)
    y_hi = lax.rem(lax.div(rep, 2), 2)
    z = lax.div(rep, 4)
    hi, lo = lax.div(fsdp, 4), lax.rem(fsdp, 4)
    u = lax.div(lo, 2)
    half = hi + core * (lo + u * (3 - 2 * lo) - hi)
    pos = lo + core * (hi + u * (3 - 2 * hi) - lo)
    odd = lax.rem(pos, 2)
    slot_pos = [pos, lax.rem(pos + 3 + 2 * odd, 4), lax.rem(pos + 1 + 2 * odd, 4), lax.rem(pos + 2, 4)]
    mine = [ring_index(core, half, s) for s in slot_pos]
    theirs = [ring_index(core, 1 - half, s) for s in slot_pos]
    to_a, to_b, partner = {"fsdp": mine[1]}, {"fsdp": mine[2]}, {"fsdp": theirs[0]}

    def rep_peer(z_, y_, c_):
        return {"rep": z_ * 4 + y_ * 2 + c_}

    bit1, bit2, bit4 = lax.rem(z, 2), lax.rem(lax.div(z, 2), 2), lax.div(z, 4)
    sibling = rep_peer(z, y_hi, 1 - core)
    z_one = rep_peer(z + 1 - 2 * bit1, y_hi, core)
    z_two = rep_peer(z + 2 - 4 * bit2, y_hi, core)
    z_four = rep_peer(z + 4 - 8 * bit4, y_hi, core)
    across = rep_peer(z, 1 - y_hi, core)

    counts = {"remote": 0, "local": 0}
    loaded = set()

    def remote(src, dst, device):
        n = counts["remote"]
        counts["remote"] = n + 1
        return pltpu.make_async_remote_copy(
            src_ref=src, dst_ref=dst, send_sem=send.at[n], recv_sem=recv.at[n],
            device_id=device, device_id_type=MESH,
        )

    def nearby(src, dst):
        n = counts["local"]
        counts["local"] = n + 1
        return pltpu.make_async_copy(src, dst, local.at[n])

    def columns(i):
        return pl.ds(pl.multiple_of(i * BLK, BLK), BLK)

    keys, values = pl.ds(0, HEAD_DIM), pl.ds(HEAD_DIM, HEAD_DIM)
    own, other = pl.ds(0, TOK), pl.ds(TOK, TOK)
    low, high = pl.ds(0, VIA_B), pl.ds(VIA_B, BLK - VIA_B)

    load_w = [
        [
            nearby(w.at[0, :, pl.ds(k * HEAD_DIM, HEAD_DIM)], WG.at[k, 0, :, keys]),
            nearby(w.at[0, :, pl.ds((KV_HEADS + k) * HEAD_DIM, HEAD_DIM)], WG.at[k, 0, :, values]),
        ]
        for k in range(KV_HEADS)
    ]
    load_x = [nearby(lat.at[0, :, columns(mine[s])], X.at[s, own, :]) for s in range(4)]
    load_act, load_table = nearby(act, SA), nearby(table, TB)
    load_delta = nearby(delta.at[0], DL)
    load_q, load_c = nearby(q.at[0], QV), nearby(cot.at[0], CV)
    load_m, load_a = nearby(mom, MO), nearby(anc, AN)
    for k in (1, 2):
        for c in load_w[k]:
            c.start()
    load_delta.start()
    load_act.start()
    load_table.start()

    lat_send = [
        remote(lat.at[0, :, columns(theirs[s])], X.at[s, other, :], partner) for s in range(4)
    ]
    w_a = [remote(WG.at[k, 0], WG.at[k, 1], to_a) for k in range(KV_HEADS)]
    w_b = [remote(WG.at[k, 0], WG.at[k, 2], to_b) for k in range(KV_HEADS)]
    w_ba = [remote(WG.at[k, 2], WG.at[k, 3], to_a) for k in range(KV_HEADS)]
    kv_send = [remote(KS.at[k], KR.at[k], partner) for k in range(KV_HEADS)]
    g_send = [remote(G.at[k, own, :], G.at[k, other, :], partner) for k in range(KV_HEADS)]
    opp_a = [remote(S3.at[k, high], OA.at[k], to_a) for k in range(KV_HEADS)]
    opp_b = [remote(S3.at[k, low], OB.at[k], to_b) for k in range(KV_HEADS)]
    sum_b_low = [remote(S2.at[k, low], RB.at[k, low], to_b) for k in range(KV_HEADS)]
    sum_b_high = [remote(S2.at[k, high], RB.at[k, high], to_b) for k in range(KV_HEADS)]
    sum_a_low = [remote(S1.at[k, low], RA.at[k, low], to_a) for k in range(KV_HEADS)]
    sum_a_high = [remote(S1.at[k, high], RA.at[k, high], to_a) for k in range(KV_HEADS)]

    rows_mine = pl.ds(pl.multiple_of(core * 16, 16), 16)
    rows_other = pl.ds(pl.multiple_of((1 - core) * 16, 16), 16)

    def cols_at(start, width):
        return pl.ds(pl.multiple_of(start, 256), width)

    c1 = bit1 * 2048
    c2 = c1 + bit2 * 1024
    c4 = c2 + bit4 * 512
    cy = c4 + y_hi * 256
    o1 = (1 - bit1) * 2048
    o2 = c1 + (1 - bit2) * 1024
    o4 = c2 + (1 - bit4) * 512
    oy = c4 + (1 - y_hi) * 256
    halve = [
        remote(DL.at[rows_other, :], CR, sibling),
        remote(AC.at[:, cols_at(o1, 2048)], R1, z_one),
        remote(AC.at[:, cols_at(o2, 1024)], R2, z_two),
        remote(AC.at[:, cols_at(o4, 512)], R3, z_four),
        remote(AC.at[:, cols_at(oy, 256)], R4, across),
    ]
    double = [
        remote(FU.at[rows_mine, cols_at(s, n)], FU.at[rows_mine, cols_at(s, n)], d)
        for s, n, d in ((cy, 256, across), (c4, 512, z_four), (c2, 1024, z_two), (c1, 2048, z_one))
    ]
    double.append(remote(FU.at[rows_mine, :], FU.at[rows_mine, :], sibling))

    bits = [None, bit1, bit2, bit4, y_hi]

    def outer_offer(step):
        @pl.when(bits[step] == 1)
        def _():
            halve[step].start()

    def outer_answer(step):
        @pl.when(bits[step] == 0)
        def _():
            halve[step].wait_recv()
            halve[step].start()

    def outer_halve(step):
        if step == 0:
            halve[0].wait_recv()
            AC[...] = DL[rows_mine, :] + CR[...]
        else:

            @pl.when(bits[step] == 1)
            def _():
                halve[step].wait_recv()

            start, width, got = ((c1, 2048, R1), (c2, 1024, R2), (c4, 512, R3), (cy, 256, R4))[step - 1]
            total = AC[:, cols_at(start, width)] + got[...]
            if step < 4:
                AC[:, cols_at(start, width)] = total
            else:
                FU[rows_mine, cols_at(start, width)] = total
        if step < 4:
            outer_offer(step + 1)
        else:
            double[0].start()

    def outer_double(step):
        double[step].wait_recv()
        if step < 4:
            double[step + 1].start()

    def outer_update():
        load_m.wait()
        load_a.wait()
        average = FU[...] * f32(1.0 / 32.0)
        momentum = f32(MOMENTUM_RATE) * MO[...] + average
        nm_out[...] = momentum
        na_out[...] = AN[...] - f32(OUTER_RATE) * (average + f32(MOMENTUM_RATE) * momentum)

    def build_mask():
        t_at = lax.broadcasted_iota(jnp.int32, (CH, CH), 0)
        f_at = lax.broadcasted_iota(jnp.int32, (CH, CH), 1)
        seen = (lax.shift_right_logical(t_at, 4) == lax.shift_right_logical(f_at, 4)) & (t_at <= f_at)
        one = jnp.where(seen, f32(1.0), f32(0.0))
        for j in range(GROUP):
            MK[:, pl.ds(j * CH, CH)] = one

    def embed():
        load_act.wait()
        load_table.wait()
        frame = lax.broadcasted_iota(jnp.int32, (FRAMES, BLK), 0)
        chosen = jnp.zeros((FRAMES, BLK), jnp.int32)
        for f in range(FRAMES):
            chosen = jnp.where(frame == f, SA[0, f], chosen)
        for s in range(4):
            rows = TB[:, columns(mine[s])].astype(f32)
            shift = jnp.zeros((FRAMES, BLK), f32)
            for a in range(ACTIONS):
                shift = jnp.where(chosen == a, rows[a : a + 1, :], shift)
            EM[s] = shift

    def condition(s, base):
        shift = EM[s]

        def chunk(i, _):
            rows = pl.ds(pl.multiple_of(base + i * 64, 64), 64)
            wide = X[s, rows, :].astype(f32).reshape(4, FRAMES, BLK) + shift[None]
            X[s, rows, :] = wide.reshape(64, BLK).astype(bf16)
            return 0

        lax.fori_loop(0, TOK // 64, chunk, 0)

    def transpose(s, base):
        def chunk(i, _):
            rows = pl.ds(pl.multiple_of(base + i * 128, 128), 128)
            XT[s, :, rows] = X[s, rows, :].T
            return 0

        lax.fori_loop(0, TOK // 128, chunk, 0)

    def project(k, rows):
        total = jnp.dot(X[0, rows, :], WG[k, 0], preferred_element_type=f32)
        for s in range(1, 4):
            total += jnp.dot(X[s, rows, :], WG[k, s], preferred_element_type=f32)
        return total

    def project_other(k):
        KS[k] = project(k, other).astype(bf16)
        kv_send[k].start()

    def condition_own(s):
        load_x[s].wait()
        condition(s, 0)

    def condition_other(s):
        lat_send[s].wait_recv()
        condition(s, TOK)

    def project_first(s):
        part = jnp.dot(X[s, other, :], WG[0, s], preferred_element_type=f32)
        if s == 0:
            G0[0] = part
        elif s < 3:
            G0[0] += part
        else:
            KS[0] = (G0[0] + part).astype(bf16)
            kv_send[0].start()

    def project_own(k):
        O[k] = project(k, own)

    def send_w(k, copy):
        if k not in loaded:
            loaded.add(k)
            for c in load_w[k]:
                c.wait()
        copy.start()

    def forward_ba(k):
        w_b[k].wait_recv()
        w_ba[k].start()

    def have_w(k):
        w_a[k].wait_recv()
        w_ba[k].wait_recv()

    def attention(k):
        kv_send[k].wait_recv()
        scale = HEAD_DIM**-0.5
        nt = (((1,), (1,)), ((), ()))

        def block(b, _):
            rows = pl.ds(pl.multiple_of(b * CH, CH), CH)
            kv = (O[k, rows, :] + KR[k, rows, :].astype(f32)).astype(bf16)
            key, value = kv[:, :HEAD_DIM], kv[:, HEAD_DIM:]
            heads = [pl.ds((k * GROUP + j) * HEAD_DIM, HEAD_DIM) for j in range(GROUP)]
            query = jnp.concatenate([QV[rows, h] for h in heads], axis=0)
            up = jnp.concatenate([CV[rows, h] for h in heads], axis=0)
            keep = MK[...] > 0.0
            scores = lax.dot_general(key, query, nt, preferred_element_type=f32)
            scores = jnp.where(keep, scores, f32(-1e30))
            top = jnp.max(scores, axis=0, keepdims=True)
            grown = jnp.exp2((scores - top) * f32(scale * LOG2E))
            probs = grown * (1.0 / jnp.sum(grown, axis=0, keepdims=True))
            prob_grad = lax.dot_general(value, up, nt, preferred_element_type=f32)
            mean = jnp.sum(probs * prob_grad, axis=0, keepdims=True)
            score_grad = (probs * (prob_grad - mean)).astype(bf16)
            G[k, rows, values] = jnp.dot(
                probs.astype(bf16), up, preferred_element_type=f32
            ).astype(bf16)
            G[k, rows, keys] = (
                jnp.dot(score_grad, query, preferred_element_type=f32) * f32(scale)
            ).astype(bf16)
            return 0

        lax.fori_loop(0, TOK // CH, block, 0, unroll=4)
        g_send[k].start()

    def gradient_opposite(k):
        g_send[k].wait_recv()
        S3[k] = jnp.dot(XT[3], G[k], preferred_element_type=f32).astype(bf16)
        opp_a[k].start()
        opp_b[k].start()

    def gradient_a(k):
        part = jnp.dot(XT[1], G[k], preferred_element_type=f32)
        T1[k] = part[:VIA_B]
        S1[k, high] = part[VIA_B:].astype(bf16)
        sum_a_high[k].start()

    def gradient_b(k):
        part = jnp.dot(XT[2], G[k], preferred_element_type=f32)
        T2[k] = part[VIA_B:]
        S2[k, low] = part[:VIA_B].astype(bf16)
        sum_b_low[k].start()

    def gradient_own(k):
        G0[k] = jnp.dot(XT[0], G[k], preferred_element_type=f32)

    def relay_to_b(k):
        opp_a[k].wait_recv()
        S2[k, high] = (T2[k] + OA[k].astype(f32)).astype(bf16)
        sum_b_high[k].start()

    def relay_to_a(k):
        opp_b[k].wait_recv()
        S1[k, low] = (T1[k] + OB[k].astype(f32)).astype(bf16)
        sum_a_low[k].start()

    def finish(k):
        for c in (sum_a_low[k], sum_a_high[k], sum_b_low[k], sum_b_high[k]):
            c.wait_recv()
        total = (G0[k] + RA[k].astype(f32) + RB[k].astype(f32)).astype(bf16)
        wg_out[0, :, pl.ds(k * HEAD_DIM, HEAD_DIM)] = total[:, :HEAD_DIM]
        wg_out[0, :, pl.ds((KV_HEADS + k) * HEAD_DIM, HEAD_DIM)] = total[:, HEAD_DIM:]

    barrier = pltpu.get_barrier_semaphore()
    peers = (partner, to_a, to_b, sibling)
    for peer in peers:
        pl.semaphore_signal(barrier, inc=1, device_id=peer, device_id_type=MESH)
    for bit, peer in ((bit1, z_one), (bit2, z_two), (bit4, z_four), (y_hi, across)):

        @pl.when(bit == 0)
        def _():
            pl.semaphore_signal(barrier, inc=1, device_id=peer, device_id_type=MESH)

    pl.semaphore_wait(barrier, len(peers) + bit1 + bit2 + bit4 + y_hi)

    send_w(1, w_b[1])
    send_w(1, w_a[1])
    embed()
    lat_send[3].start()
    send_w(2, w_a[2])
    load_delta.wait()
    halve[0].start()
    for c in load_x:
        c.start()
    for k in (0, 3):
        for c in load_w[k]:
            c.start()
    outer_halve(0)
    lat_send[0].start()
    build_mask()
    lat_send[1].start()
    send_w(2, w_b[2])
    condition_own(3)
    forward_ba(1)
    for c in (load_q, load_c):
        c.start()
    outer_answer(1)
    outer_halve(1)
    lat_send[2].start()
    condition_own(0)
    send_w(3, w_a[3])
    forward_ba(2)
    for c in (load_m, load_a):
        c.start()
    outer_answer(2)
    outer_halve(2)
    condition_own(2)
    send_w(0, w_b[0])
    condition_own(1)
    transpose(1, 0)
    send_w(0, w_a[0])
    send_w(3, w_b[3])
    outer_answer(3)
    have_w(1)
    transpose(0, 0)
    condition_other(3)
    condition_other(1)
    outer_halve(3)
    transpose(2, 0)
    condition_other(2)
    condition_other(0)
    have_w(2)
    project_own(2)
    transpose(3, TOK)
    project_other(2)
    outer_answer(4)
    forward_ba(0)
    project_own(1)
    project_other(1)
    load_q.wait()
    load_c.wait()
    attention(2)
    forward_ba(3)
    transpose(3, 0)
    outer_halve(4)
    have_w(0)
    project_first(0)
    attention(1)
    project_first(1)
    gradient_opposite(2)
    transpose(1, TOK)
    project_first(2)
    project_first(3)
    gradient_a(2)
    project_own(0)
    have_w(3)
    project_other(3)
    gradient_opposite(1)
    project_own(3)
    transpose(2, TOK)
    gradient_a(1)
    relay_to_a(2)
    outer_double(0)
    attention(0)
    transpose(0, TOK)
    relay_to_a(1)
    attention(3)
    gradient_opposite(0)
    gradient_b(2)
    outer_double(1)
    gradient_a(0)
    gradient_own(0)
    gradient_opposite(3)
    gradient_a(3)
    gradient_b(0)
    relay_to_b(2)
    gradient_b(3)
    outer_double(2)
    gradient_own(2)
    relay_to_a(0)
    relay_to_a(3)
    relay_to_b(0)
    gradient_b(1)
    gradient_own(3)
    relay_to_b(1)
    outer_double(3)
    finish(2)
    outer_double(4)
    outer_update()
    finish(0)
    gradient_own(1)
    relay_to_b(3)
    finish(1)
    finish(3)

    for group in (
        lat_send, w_a, w_b, w_ba, kv_send, g_send, opp_a, opp_b,
        sum_a_low, sum_a_high, sum_b_low, sum_b_high, halve, double,
    ):
        for c in group:
            c.wait_send()


def body(
    latent_tokens,
    actions,
    action_table,
    key_value_weight,
    queries,
    output_cotangent,
    outer_delta,
    momentum,
    anchor,
):
    f32, bf16 = jnp.float32, jnp.bfloat16
    H = KV_HEADS
    vm = pltpu.VMEM
    scratch = [
        vm((4, 2 * TOK, BLK), bf16),
        vm((4, BLK, 2 * TOK), bf16),
        vm((H, 4, BLK, HW), bf16),
        vm((TOK, 2048), bf16),
        vm((TOK, 2048), bf16),
        vm((ACTIONS, 4096), bf16),
        pltpu.SMEM((1, FRAMES), jnp.int32),
        vm((4, FRAMES, BLK), f32),
        vm((CH, GROUP * CH), f32),
        vm((H, TOK, HW), f32),
        vm((H, TOK, HW), bf16),
        vm((H, TOK, HW), bf16),
        vm((H, 2 * TOK, HW), bf16),
        vm((H, BLK, HW), bf16),
        vm((H, BLK, HW), bf16),
        vm((H, BLK, HW), bf16),
        vm((H, BLK - VIA_B, HW), f32),
        vm((H, VIA_B, HW), f32),
        vm((H, BLK, HW), f32),
        vm((H, BLK - VIA_B, HW), bf16),
        vm((H, VIA_B, HW), bf16),
        vm((H, BLK, HW), bf16),
        vm((H, BLK, HW), bf16),
        vm((32, 4096), f32),
        vm((16, 4096), f32),
        vm((16, 4096), f32),
        vm((16, 2048), f32),
        vm((16, 1024), f32),
        vm((16, 512), f32),
        vm((16, 256), f32),
        vm((32, 4096), f32),
        vm((32, 4096), f32),
        vm((32, 4096), f32),
        pltpu.SemaphoreType.DMA((58,)),
        pltpu.SemaphoreType.DMA((58,)),
        pltpu.SemaphoreType.DMA((24,)),
    ]
    hbm = pl.BlockSpec(memory_space=pl.ANY)
    vmem = pl.BlockSpec(memory_space=pltpu.VMEM)
    return pl.pallas_call(
        kernel,
        out_shape=(
            vm((1, BLK, 2 * H * HEAD_DIM), bf16),
            vm((32, 4096), f32),
            vm((32, 4096), f32),
        ),
        in_specs=[hbm] * 9,
        out_specs=(vmem, vmem, vmem),
        scratch_shapes=scratch,
        compiler_params=pltpu.CompilerParams(
            collective_id=0, has_side_effects=True, vmem_limit_bytes=56 * 2**20
        ),
        cost_estimate=pl.CostEstimate(
            flops=10 * 10**9, bytes_accessed=16 * 2**20, transcendentals=10**6
        ),
    )(
        latent_tokens, actions, action_table, key_value_weight, queries, output_cotangent,
        outer_delta, momentum, anchor,
    )


def solution(mesh):
    return jax.shard_map(
        body,
        mesh=mesh,
        in_specs=(
            P("rep", "fsdp", None),
            P("rep", None),
            P(),
            P("rep", "fsdp", None),
            P("rep", "fsdp", None),
            P("rep", "fsdp", None),
            P("rep", "fsdp", None),
            P("fsdp", None),
            P("fsdp", None),
        ),
        out_specs=(P("rep", "fsdp", None), P("fsdp", None), P("fsdp", None)),
        check_vma=False,
    )
```
